256 devices in a mesh: dp: 8 (over z), ctx: 32 (over x, y, core).
Axes of the slice: x: 4, y: 4, z: 8, core: 2. Of those that a mesh axis runs over, the one named last changes fastest.
Arguments:
- queries: bfloat16 [16, 4096, 512], P('dp', 'ctx'), may hold values from -40 to 40
- keys: bfloat16 [16, 4096, 128], P('dp', 'ctx'), may hold values from -18 to 18
- values: bfloat16 [16, 4096, 128], P('dp', 'ctx'), may hold values from -6 to 6
- upstream: bfloat16 [16, 4096, 512], P('dp', 'ctx'), may hold values from -6 to 6
- doc_ids: int32 [16, 4096], P('dp'), may hold values from 0 to 31, as said below
Outputs:
- attn_out: bfloat16 [16, 4096, 512], P('dp', 'ctx')
- grad_query: bfloat16 [16, 4096, 512], P('dp', 'ctx')
- grad_key: bfloat16 [16, 4096, 128], P('dp', 'ctx')
- grad_value: bfloat16 [16, 4096, 128], P('dp', 'ctx')
The draws below stay inside these ranges and needn't reach their ends.
Inputs may be any that keep to these rules, and one draw needn't show every extreme that they name: `doc_ids`: ids never fall along a pack; document 0 holds exactly 256 tokens and every other document 1 to 256 tokens.
All inputs are finite; a program needn't handle non-finite values.
Results may differ from the reference program's by a relative error of at most 0.013.
Values may be sent and summed in bfloat16 or wider, within the bound.
A program may use at most 64 MiB of HBM per device.

```python
import jax
import jax.numpy as jnp
from jax import lax

HEADS = 4
HD = 128
TOK_DEV = 128
WINDOW = 4096
PACKS = 16
MOST = 256
DOCS = 32


def shared_base(key):
    base = jax.random.normal(key, (PACKS, WINDOW, HD), jnp.float32)
    return jnp.clip(base, -6.0, 6.0)


def draw_keys(key, part):
    base = shared_base(key)
    return base.astype(jnp.bfloat16)


def draw_queries(key, part):
    key = jax.random.fold_in(key, 13)
    own_draw = jnp.clip(jax.random.normal(key, (PACKS, WINDOW, HEADS * HD), jnp.float32), -6.0, 6.0)
    return own_draw.astype(jnp.bfloat16)


def draw_doc_ids(key, part):
    key = jax.random.fold_in(key, 21)
    rest_rows = WINDOW - MOST
    order = jnp.arange(1, DOCS - 1, dtype=jnp.int32)
    jitter = jax.random.randint(key, (PACKS, DOCS - 2), -(TOK_DEV // 4), TOK_DEV // 4 + 1, dtype=jnp.int32)
    starts = MOST + order * rest_rows // (DOCS - 1) + jitter
    positions = jnp.arange(WINDOW, dtype=jnp.int32)
    later = (positions[None, :, None] >= starts[:, None, :]).astype(jnp.int32)
    first_cut = (positions >= MOST).astype(jnp.int32)
    return first_cut[None, :] + jnp.sum(later, axis=2)


def level_of(rng, shape, split, least, largest):
    level = 1.0
    for dim, blocks in split:
        draws = jax.random.uniform(jax.random.fold_in(jax.random.fold_in(rng, 6), dim), (blocks,), jnp.float32, least / len(split), largest / len(split))
        level = level * jnp.repeat(jnp.exp(draws), shape[dim] // blocks).reshape((-1,) + (1,) * (len(shape) - 1 - dim))
    return level


def noise(key, dims, scale, bound, shards=(), kind=jnp.bfloat16):
    array = scale * jax.random.normal(key, dims, jnp.float32)
    if shards:
        array = array * level_of(key, dims, shards, -0.22, 0.18)
    return jnp.clip(array, -bound, bound).astype(kind)


def setup_inputs(seed: int = 0) -> dict:
    streams_of = jax.random.split(jax.random.key(seed), 6)
    return {
        "queries": draw_queries(jax.random.fold_in(streams_of[5], 71), 0),
        "keys": draw_keys(jax.random.fold_in(streams_of[5], 71), 0),
        "values": noise(streams_of[2], (PACKS, WINDOW, HD), 1.0, 6.0, ((0, 8), (1, 32))),
        "upstream": noise(streams_of[3], (PACKS, WINDOW, HEADS * HD), 1.0, 6.0, ((0, 8), (1, 32))),
        "doc_ids": draw_doc_ids(jax.random.fold_in(streams_of[5], 71), 0),
    }


NEG_LARGE = -1.0e30


def one_pack(operands):
    queries, keys, values, upstream, doc_ids = operands
    head_dim = keys.shape[1]
    head_count = queries.shape[1] // head_dim
    score_scale = head_dim ** -0.5
    span_rows = MOST + TOK_DEV
    query_heads = queries.reshape(WINDOW, head_count, head_dim)
    upward = upstream.reshape(WINDOW, head_count, head_dim)
    row_index = jnp.arange(TOK_DEV, dtype=jnp.int32)
    key_index = jnp.arange(span_rows, dtype=jnp.int32)

    def block_step(carried, block):
        key_grad, value_grad = carried
        first_row = (block * TOK_DEV).astype(jnp.int32)
        key_first = jnp.maximum(first_row - MOST, 0).astype(jnp.int32)
        query_blk = lax.dynamic_slice_in_dim(query_heads, first_row, TOK_DEV, 0).astype(jnp.float32)
        upward_blk = lax.dynamic_slice_in_dim(upward, first_row, TOK_DEV, 0).astype(jnp.float32)
        key_blk = lax.dynamic_slice_in_dim(keys, key_first, span_rows, 0).astype(jnp.float32)
        value_blk = lax.dynamic_slice_in_dim(values, key_first, span_rows, 0).astype(jnp.float32)
        query_ids = lax.dynamic_slice_in_dim(doc_ids, first_row, TOK_DEV, 0)
        key_ids = lax.dynamic_slice_in_dim(doc_ids, key_first, span_rows, 0)
        same_doc = query_ids[:, None] == key_ids[None, :]
        causal = (key_first + key_index)[None, :] <= (first_row + row_index)[:, None]
        allowed = (same_doc & causal)[None, :, :]
        scores = jnp.einsum("thd,sd->hts", query_blk, key_blk) * score_scale
        masked = jnp.where(allowed, scores, NEG_LARGE)
        row_peak = jnp.max(masked, axis=-1, keepdims=True)
        log_total = row_peak + jnp.log(jnp.sum(jnp.exp(masked - row_peak), axis=-1, keepdims=True))
        prob = jnp.where(allowed, jnp.exp(masked - log_total), 0.0)
        prob_low = lax.optimization_barrier(prob.astype(jnp.bfloat16)).astype(jnp.float32)
        attn_blk = jnp.einsum("hts,sd->thd", prob_low, value_blk)
        slopes = jnp.einsum("thd,sd->hts", upward_blk, value_blk)
        row_delta = jnp.sum(prob * slopes, axis=-1, keepdims=True)
        dscore = prob * (slopes - row_delta)
        dscore_low = lax.optimization_barrier(dscore.astype(jnp.bfloat16)).astype(jnp.float32)
        query_grad = jnp.einsum("hts,sd->thd", dscore_low, key_blk) * score_scale
        key_part = jnp.einsum("hts,thd->sd", dscore_low, query_blk)
        value_part = jnp.einsum("hts,thd->sd", prob_low, upward_blk)
        key_grad = lax.dynamic_update_slice_in_dim(
            key_grad, lax.dynamic_slice_in_dim(key_grad, key_first, span_rows, 0) + key_part, key_first, 0)
        value_grad = lax.dynamic_update_slice_in_dim(
            value_grad, lax.dynamic_slice_in_dim(value_grad, key_first, span_rows, 0) + value_part, key_first, 0)
        return (key_grad, value_grad), (attn_blk.astype(jnp.bfloat16), query_grad.astype(jnp.bfloat16))

    start_grads = (jnp.zeros((WINDOW, head_dim), jnp.float32), jnp.zeros((WINDOW, head_dim), jnp.float32))
    block_list = jnp.arange(WINDOW // TOK_DEV, dtype=jnp.int32)
    grads, stacked = lax.scan(block_step, start_grads, block_list)
    attn_out = stacked[0].reshape(WINDOW, head_count * head_dim)
    grad_query = stacked[1].reshape(WINDOW, head_count * head_dim)
    return attn_out, grad_query, grads[0], grads[1]


def reference(queries, keys, values, upstream, doc_ids):
    score_scale = HD ** -0.5
    attn_out, grad_query, key_grad, value_grad = lax.map(one_pack, (queries, keys, values, upstream, doc_ids))
    grad_key = (key_grad * score_scale).astype(jnp.bfloat16)
    grad_value = value_grad.astype(jnp.bfloat16)
    return attn_out, grad_query, grad_key, grad_value
```

```python
import math

import jax
import jax.numpy as jnp
from jax import lax
from jax.experimental import pallas as pl
from jax.experimental.pallas import tpu as pltpu
from jax.sharding import PartitionSpec as P

MESH = pl.DeviceIdType.MESH
NEG_LARGE = -1e30
HEAD = 128


def nt(a, b):
    return lax.dot_general(a, b, (((1,), (1,)), ((), ())), preferred_element_type=jnp.float32)


def nn(a, b):
    return lax.dot_general(a, b, (((1,), (0,)), ((), ())), preferred_element_type=jnp.float32)


def stacked(ref, block, heads):
    return jnp.concatenate(
        [ref[block, :, h * HEAD : (h + 1) * HEAD] for h in range(heads)], axis=0
    )


def kernel(
    q_hbm, k_hbm, v_hbm, u_hbm, ids_hbm,
    out_hbm, gq_hbm, gk_hbm, gv_hbm,
    q_all, u_all, k_all, v_all, ids_v, bias,
    e_loc, d_loc, p_low, s_low,
    gk_send, gv_send, gk_in, gv_in, gk_mate, gv_mate, gk_mine, gv_mine, gk_fin, gv_fin,
    out_buf, gq_buf,
    load_sem, ids_sem, kv_send, kv_recv, mate_send, mate_recv,
    g_send, g_recv, gm_send, gm_recv, o_send, o_recv, store_sem, fin_sem,
):
    tok = q_all.shape[1]
    heads = q_all.shape[2] // HEAD
    scale = HEAD**-0.5
    log2_scale = scale * math.log2(math.e)
    ctx = lax.axis_index("ctx")
    dp = lax.axis_index("dp")
    chips = lax.axis_size("ctx") // 2
    chip = ctx // 2
    core = ctx % 2
    peer = 1 - core
    mate = chip * 2 + peer
    later = lax.rem(chip + 1, chips)
    earlier = lax.rem(chip + chips - 1, chips)

    def remote(src, dst, send, recv, target):
        return pltpu.make_async_remote_copy(
            src_ref=src, dst_ref=dst, send_sem=send, recv_sem=recv,
            device_id=(dp, target), device_id_type=MESH,
        )

    barrier = pltpu.get_barrier_semaphore()
    for target in (earlier * 2, earlier * 2 + 1, mate):
        pl.semaphore_signal(barrier, inc=1, device_id=(dp, target), device_id_type=MESH)

    loads = [
        pltpu.make_async_copy(q_hbm.at[core], q_all.at[core], load_sem.at[0]),
        pltpu.make_async_copy(u_hbm.at[core], u_all.at[core], load_sem.at[1]),
        pltpu.make_async_copy(k_hbm.at[core], k_all.at[2 + core], load_sem.at[2]),
        pltpu.make_async_copy(v_hbm.at[core], v_all.at[2 + core], load_sem.at[3]),
        pltpu.make_async_copy(
            ids_hbm.at[:, pl.ds(pl.multiple_of(earlier * 2 * tok, 2 * tok), 2 * tok)],
            ids_v.at[:, pl.ds(0, 2 * tok)], ids_sem.at[0],
        ),
        pltpu.make_async_copy(
            ids_hbm.at[:, pl.ds(pl.multiple_of(chip * 2 * tok, 2 * tok), 2 * tok)],
            ids_v.at[:, pl.ds(2 * tok, 2 * tok)], ids_sem.at[1],
        ),
    ]
    for copy in loads:
        copy.start()

    pl.semaphore_wait(barrier, 3)

    kv_out = []
    for pack in range(2):
        target = later * 2 + pack
        kv_out += [
            remote(k_hbm.at[pack], k_all.at[core], kv_send.at[pack, 0], kv_recv.at[core, 0], target),
            remote(v_hbm.at[pack], v_all.at[core], kv_send.at[pack, 1], kv_recv.at[core, 1], target),
        ]
    mate_out = [
        remote(k_hbm.at[peer], k_all.at[2 + core], mate_send.at[0], mate_recv.at[0], mate),
        remote(v_hbm.at[peer], v_all.at[2 + core], mate_send.at[1], mate_recv.at[1], mate),
        remote(q_hbm.at[peer], q_all.at[core], mate_send.at[2], mate_recv.at[2], mate),
        remote(u_hbm.at[peer], u_all.at[core], mate_send.at[3], mate_recv.at[3], mate),
    ]
    for copy in kv_out + mate_out:
        copy.start()

    for copy in loads[4:]:
        copy.wait()
    ids_two = ids_v[...]
    ids_row = jnp.where(core == 0, ids_two[0:1], ids_two[1:2])
    lane = lax.broadcasted_iota(jnp.int32, ids_row.shape, 1)
    ids_row = jnp.where((lane < 2 * tok) & (chip == 0), -1, ids_row)
    ids_col = jnp.transpose(jnp.broadcast_to(ids_row, (tok, 4 * tok)))
    for block in range(2):
        first = block * tok
        q_first = (2 + block) * tok
        key_pos = first + lax.broadcasted_iota(jnp.int32, (3 * tok, tok), 0)
        query_pos = q_first + lax.broadcasted_iota(jnp.int32, (3 * tok, tok), 1)
        allowed = (ids_col[first : first + 3 * tok] == ids_row[:, q_first : q_first + tok]) & (
            key_pos <= query_pos
        )
        bias[block] = jnp.where(allowed, 0.0, NEG_LARGE)

    for copy in loads[:4]:
        copy.wait()
    mate_in = [
        remote(k_hbm.at[core], k_all.at[2 + peer], mate_send.at[0], mate_recv.at[0], mate),
        remote(v_hbm.at[core], v_all.at[2 + peer], mate_send.at[1], mate_recv.at[1], mate),
        remote(q_hbm.at[core], q_all.at[peer], mate_send.at[2], mate_recv.at[2], mate),
        remote(u_hbm.at[core], u_all.at[peer], mate_send.at[3], mate_recv.at[3], mate),
    ]
    for copy in mate_in:
        copy.wait_recv()

    def tile(block, key_first, key_blocks):
        span = key_blocks * tok
        keys = k_all[key_first : key_first + key_blocks].reshape(span, HEAD)
        vals = v_all[key_first : key_first + key_blocks].reshape(span, HEAD)
        row = (key_first - block) * tok
        add = bias[block, row : row + span]
        scores = nt(keys, stacked(q_all, block, heads))
        slopes = nt(vals, stacked(u_all, block, heads))
        scores = scores * log2_scale + jnp.concatenate([add] * heads, axis=1)
        return scores, slopes

    local = []
    for block in range(2):
        span = (block + 1) * tok
        scores, slopes = tile(block, 2, block + 1)
        peak = jnp.max(scores, axis=0, keepdims=True)
        weights = jnp.exp2(scores - peak)
        e_loc[block, :span] = weights
        d_loc[block, :span] = slopes
        total = jnp.sum(weights, axis=0, keepdims=True)
        weighted = jnp.sum(weights * slopes, axis=0, keepdims=True)
        local.append((peak, total, weighted))

    for block in range(2):
        for array in range(2):
            ref = (k_all, v_all)[array]
            remote(
                (k_hbm, v_hbm)[array].at[0], ref.at[block],
                kv_send.at[0, array], kv_recv.at[block, array], mate,
            ).wait_recv()

    stats = []
    back = []
    carry_k = carry_v = None
    for block in range(2):
        span = (2 - block) * tok
        scores, slopes = tile(block, block, 2 - block)
        peak, total, weighted = local[block]
        new_peak = jnp.maximum(peak, jnp.max(scores, axis=0, keepdims=True))
        factor = jnp.exp2(peak - new_peak)
        weights = jnp.exp2(scores - new_peak)
        total = total * factor + jnp.sum(weights, axis=0, keepdims=True)
        weighted = weighted * factor + jnp.sum(weights * slopes, axis=0, keepdims=True)
        inverse = 1.0 / total
        delta = weighted * inverse
        stats.append((factor * inverse, delta))
        prob = weights * inverse
        prob_b = prob.astype(jnp.bfloat16)
        slope_b = (prob * (slopes - delta)).astype(jnp.bfloat16)
        p_low[block, :span] = prob_b
        s_low[block, :span] = slope_b
        part_v = nn(prob_b, stacked(u_all, block, heads))
        part_k = nn(slope_b, stacked(q_all, block, heads))
        if block == 0:
            carry_k, carry_v = part_k[tok:], part_v[tok:]
            done_k, done_v = part_k[:tok], part_v[:tok]
        else:
            done_k, done_v = carry_k + part_k, carry_v + part_v
        gk_send[block] = done_k.astype(jnp.bfloat16)
        gv_send[block] = done_v.astype(jnp.bfloat16)
        target = earlier * 2 + block
        for copy in (
            remote(gk_send.at[block], gk_in.at[core], g_send.at[block, 0], g_recv.at[core, 0], target),
            remote(gv_send.at[block], gv_in.at[core], g_send.at[block, 1], g_recv.at[core, 1], target),
        ):
            copy.start()
            back.append(copy)

    for block in range(2):
        span = (block + 1) * tok
        row = (2 - block) * tok
        scaled, delta = stats[block]
        prob = e_loc[block, :span] * scaled
        prob_b = prob.astype(jnp.bfloat16)
        slope_b = (prob * (d_loc[block, :span] - delta)).astype(jnp.bfloat16)
        p_low[block, row:] = prob_b
        s_low[block, row:] = slope_b
        part_v = nn(prob_b, stacked(u_all, block, heads))
        part_k = nn(slope_b, stacked(q_all, block, heads))
        if block == 0:
            carry_k, carry_v = part_k, part_v
        else:
            gk_mine[0] = carry_k + part_k[:tok]
            gv_mine[0] = carry_v + part_v[:tok]
            gk_mine[1] = part_k[tok:]
            gv_mine[1] = part_v[tok:]
    mates = [
        remote(gk_mine.at[peer], gk_mate, gm_send.at[0], gm_recv.at[0], mate),
        remote(gv_mine.at[peer], gv_mate, gm_send.at[1], gm_recv.at[1], mate),
    ]
    for copy in mates:
        copy.start()

    for block in range(2):
        keys = k_all[block : block + 3].reshape(3 * tok, HEAD)
        vals = v_all[block : block + 3].reshape(3 * tok, HEAD)
        out_t = nn(jnp.transpose(vals), p_low[block]).astype(jnp.bfloat16)
        gq_t = (nn(jnp.transpose(keys), s_low[block]) * scale).astype(jnp.bfloat16)
        for h in range(heads):
            cols = slice(h * HEAD, (h + 1) * HEAD)
            rows = slice(h * tok, (h + 1) * tok)
            out_buf[block, :, cols] = jnp.transpose(out_t[:, rows])
            gq_buf[block, :, cols] = jnp.transpose(gq_t[:, rows])
    outs = [
        remote(out_buf.at[peer], out_hbm.at[core], o_send.at[0], o_recv.at[0], mate),
        remote(gq_buf.at[peer], gq_hbm.at[core], o_send.at[1], o_recv.at[1], mate),
    ]
    stores = [
        pltpu.make_async_copy(out_buf.at[core], out_hbm.at[core], store_sem.at[0]),
        pltpu.make_async_copy(gq_buf.at[core], gq_hbm.at[core], store_sem.at[1]),
    ]
    for copy in outs + stores:
        copy.start()

    for copy in mates:
        copy.wait_recv()
    for pack in range(2):
        for array in range(2):
            remote(
                (gk_send, gv_send)[array].at[pack], (gk_in, gv_in)[array].at[pack],
                g_send.at[pack, array], g_recv.at[pack, array], mate,
            ).wait_recv()
    mine = pl.ds(core, 1)
    other = pl.ds(peer, 1)
    gk_fin[mine] = ((gk_mine[mine] + gk_in[mine].astype(jnp.float32)) * scale).astype(jnp.bfloat16)
    gv_fin[mine] = (gv_mine[mine] + gv_in[mine].astype(jnp.float32)).astype(jnp.bfloat16)
    gk_fin[other] = (
        (gk_mate[...][None] + gk_in[other].astype(jnp.float32)) * scale
    ).astype(jnp.bfloat16)
    gv_fin[other] = (gv_mate[...][None] + gv_in[other].astype(jnp.float32)).astype(jnp.bfloat16)
    fins = [
        pltpu.make_async_copy(gk_fin, gk_hbm, fin_sem.at[0]),
        pltpu.make_async_copy(gv_fin, gv_hbm, fin_sem.at[1]),
    ]
    for copy in fins:
        copy.start()

    for copy in kv_out + mate_out + back + mates + outs:
        copy.wait_send()
    for copy in (
        remote(out_buf.at[core], out_hbm.at[peer], o_send.at[0], o_recv.at[0], mate),
        remote(gq_buf.at[core], gq_hbm.at[peer], o_send.at[1], o_recv.at[1], mate),
    ):
        copy.wait_recv()
    for copy in stores + fins:
        copy.wait()


def per_device(queries, keys, values, upstream, doc_ids):
    packs, tok, features = queries.shape
    heads = features // HEAD
    bf16, f32 = jnp.bfloat16, jnp.float32
    wide = heads * tok
    dma = pltpu.SemaphoreType.DMA
    anywhere = pl.BlockSpec(memory_space=pltpu.HBM)
    return pl.pallas_call(
        kernel,
        out_shape=(
            jax.ShapeDtypeStruct(queries.shape, bf16),
            jax.ShapeDtypeStruct(queries.shape, bf16),
            jax.ShapeDtypeStruct(keys.shape, bf16),
            jax.ShapeDtypeStruct(keys.shape, bf16),
        ),
        in_specs=[anywhere] * 5,
        out_specs=(anywhere,) * 4,
        scratch_shapes=[
            pltpu.VMEM((2, tok, features), bf16),
            pltpu.VMEM((2, tok, features), bf16),
            pltpu.VMEM((4, tok, HEAD), bf16),
            pltpu.VMEM((4, tok, HEAD), bf16),
            pltpu.VMEM((2, 4 * tok), jnp.int32),
            pltpu.VMEM((2, 3 * tok, tok), f32),
            pltpu.VMEM((2, 2 * tok, wide), f32),
            pltpu.VMEM((2, 2 * tok, wide), f32),
            pltpu.VMEM((2, 3 * tok, wide), bf16),
            pltpu.VMEM((2, 3 * tok, wide), bf16),
            pltpu.VMEM((2, tok, HEAD), bf16),
            pltpu.VMEM((2, tok, HEAD), bf16),
            pltpu.VMEM((2, tok, HEAD), bf16),
            pltpu.VMEM((2, tok, HEAD), bf16),
            pltpu.VMEM((tok, HEAD), f32),
            pltpu.VMEM((tok, HEAD), f32),
            pltpu.VMEM((2, tok, HEAD), f32),
            pltpu.VMEM((2, tok, HEAD), f32),
            pltpu.VMEM((2, tok, HEAD), bf16),
            pltpu.VMEM((2, tok, HEAD), bf16),
            pltpu.VMEM((2, tok, features), bf16),
            pltpu.VMEM((2, tok, features), bf16),
            dma((4,)),
            dma((2,)),
            dma((2, 2)),
            dma((2, 2)),
            dma((4,)),
            dma((4,)),
            dma((2, 2)),
            dma((2, 2)),
            dma((2,)),
            dma((2,)),
            dma((2,)),
            dma((2,)),
            dma((2,)),
            dma((2,)),
        ],
        compiler_params=pltpu.CompilerParams(
            collective_id=0, has_side_effects=True, vmem_limit_bytes=62 * 1024 * 1024
        ),
        name="attention_both_ways",
    )(queries, keys, values, upstream, doc_ids)


def solution(mesh):
    return jax.shard_map(
        per_device,
        mesh=mesh,
        in_specs=(P("dp", "ctx", None),) * 4 + (P("dp", None),),
        out_specs=(P("dp", "ctx", None),) * 4,
        check_vma=False,
    )
```

```python
import math

import jax
import jax.numpy as jnp
from jax import lax
from jax.experimental import pallas as pl
from jax.experimental.pallas import tpu as pltpu
from jax.sharding import PartitionSpec as P

MESH = pl.DeviceIdType.MESH
NEG_LARGE = -1e30
HEAD = 128


def nt(a, b):
    return lax.dot_general(a, b, (((1,), (1,)), ((), ())), preferred_element_type=jnp.float32)


def nn(a, b):
    return lax.dot_general(a, b, (((1,), (0,)), ((), ())), preferred_element_type=jnp.float32)


def stacked(ref, block, heads):
    return jnp.concatenate(
        [ref[block, :, h * HEAD : (h + 1) * HEAD] for h in range(heads)], axis=0
    )


def kernel(
    q_hbm, k_hbm, v_hbm, u_hbm, ids_hbm,
    out_fin, gq_fin, gk_fin, gv_fin,
    q_all, u_all, kv_all, kv_own, ids_v, bias,
    e_loc, d_loc, p_low, s_low,
    g_back, g_in, g_mine, g_mate, out_buf, gq_buf,
    load_sem, kv_send, kv_recv, mate_send, mate_recv,
    g_send, g_recv, gm_send, gm_recv, o_send, o_recv, store_sem,
):
    tok = q_all.shape[1]
    heads = q_all.shape[2] // HEAD
    scale = HEAD**-0.5
    log2_scale = scale * math.log2(math.e)
    ctx = lax.axis_index("ctx")
    dp = lax.axis_index("dp")
    chips = lax.axis_size("ctx") // 2
    chip = ctx // 2
    core = ctx % 2
    peer = 1 - core
    mate = chip * 2 + peer
    has_later = chip < chips - 1
    has_earlier = chip > 0
    later = lax.rem(chip + 1, chips)
    earlier = lax.rem(chip + chips - 1, chips)

    def remote(src, dst, send, recv, target):
        return pltpu.make_async_remote_copy(
            src_ref=src, dst_ref=dst, send_sem=send, recv_sem=recv,
            device_id=(dp, target), device_id_type=MESH,
        )

    barrier = pltpu.get_barrier_semaphore()

    @pl.when(has_earlier)
    def _():
        for target in (earlier * 2, earlier * 2 + 1):
            pl.semaphore_signal(barrier, inc=1, device_id=(dp, target), device_id_type=MESH)

    pl.semaphore_signal(barrier, inc=1, device_id=(dp, mate), device_id_type=MESH)

    ids_first = pl.multiple_of(earlier * 2 * tok, 2 * tok)
    ids_own = pl.multiple_of(chip * 2 * tok, 2 * tok)
    pairs = [
        (k_hbm, kv_own.at[:, 0]),
        (v_hbm, kv_own.at[:, 1]),
        (ids_hbm.at[:, pl.ds(ids_first, 2 * tok)], ids_v.at[:, pl.ds(0, 2 * tok)]),
        (ids_hbm.at[:, pl.ds(ids_own, 2 * tok)], ids_v.at[:, pl.ds(2 * tok, 2 * tok)]),
        (q_hbm.at[core], q_all.at[core]),
        (u_hbm.at[core], u_all.at[core]),
        (k_hbm.at[core], kv_all.at[2 + core, 0]),
        (v_hbm.at[core], kv_all.at[2 + core, 1]),
    ]
    loads = [
        pltpu.make_async_copy(src, dst, load_sem.at[i]) for i, (src, dst) in enumerate(pairs)
    ]
    for copy in loads:
        copy.start()

    @pl.when(jnp.logical_not(has_earlier))
    def _():
        kv_all[0:2] = jnp.zeros((2,) + kv_all.shape[1:], kv_all.dtype)

    @pl.when(jnp.logical_not(has_later))
    def _():
        g_in[...] = jnp.zeros(g_in.shape, g_in.dtype)

    for copy in loads[:2]:
        copy.wait()
    pl.semaphore_wait(barrier, jnp.where(has_later, 3, 1))

    kv_out = [
        remote(kv_own.at[pack], kv_all.at[core], kv_send.at[pack], kv_recv.at[core], later * 2 + pack)
        for pack in range(2)
    ]

    @pl.when(has_later)
    def _():
        for copy in kv_out:
            copy.start()

    def mates(block_pack, place):
        return [
            remote(
                kv_own.at[block_pack], kv_all.at[2 + place], mate_send.at[0], mate_recv.at[0], mate
            ),
            remote(q_hbm.at[block_pack], q_all.at[place], mate_send.at[1], mate_recv.at[1], mate),
            remote(u_hbm.at[block_pack], u_all.at[place], mate_send.at[2], mate_recv.at[2], mate),
        ]

    mate_out = mates(peer, core)
    for copy in mate_out:
        copy.start()

    for copy in loads[2:4]:
        copy.wait()
    ids_two = ids_v[...]
    ids_row = jnp.where(core == 0, ids_two[0:1], ids_two[1:2])
    lane = lax.broadcasted_iota(jnp.int32, ids_row.shape, 1)
    ids_row = jnp.where((lane < 2 * tok) & (chip == 0), -1, ids_row)
    ids_col = jnp.transpose(jnp.broadcast_to(ids_row, (tok, 4 * tok)))
    for block in range(2):
        first = block * tok
        q_first = (2 + block) * tok
        key_pos = first + lax.broadcasted_iota(jnp.int32, (3 * tok, tok), 0)
        query_pos = q_first + lax.broadcasted_iota(jnp.int32, (3 * tok, tok), 1)
        allowed = (ids_col[first : first + 3 * tok] == ids_row[:, q_first : q_first + tok]) & (
            key_pos <= query_pos
        )
        bias[block] = jnp.where(allowed, 0.0, NEG_LARGE)

    for copy in loads[4:]:
        copy.wait()
    for copy in mates(core, peer):
        copy.wait_recv()

    def tile(block, key_first, key_blocks):
        span = key_blocks * tok
        keys = kv_all[key_first : key_first + key_blocks, 0].reshape(span, HEAD)
        vals = kv_all[key_first : key_first + key_blocks, 1].reshape(span, HEAD)
        row = (key_first - block) * tok
        add = bias[block, row : row + span]
        scores = nt(keys, stacked(q_all, block, heads))
        slopes = nt(vals, stacked(u_all, block, heads))
        scores = scores * log2_scale + jnp.concatenate([add] * heads, axis=1)
        return scores, slopes

    local = []
    for block in range(2):
        span = (block + 1) * tok
        scores, slopes = tile(block, 2, block + 1)
        peak = jnp.max(scores, axis=0, keepdims=True)
        weights = jnp.exp2(scores - peak)
        e_loc[block, :span] = weights
        d_loc[block, :span] = slopes
        total = jnp.sum(weights, axis=0, keepdims=True)
        weighted = jnp.sum(weights * slopes, axis=0, keepdims=True)
        local.append((peak, total, weighted))

    @pl.when(has_earlier)
    def _():
        for block in range(2):
            remote(
                kv_own.at[0], kv_all.at[block], kv_send.at[0], kv_recv.at[block], mate
            ).wait_recv()

    stats = []
    back = []
    carry_k = carry_v = None
    for block in range(2):
        span = (2 - block) * tok
        scores, slopes = tile(block, block, 2 - block)
        peak, total, weighted = local[block]
        new_peak = jnp.maximum(peak, jnp.max(scores, axis=0, keepdims=True))
        factor = jnp.exp2(peak - new_peak)
        weights = jnp.exp2(scores - new_peak)
        total = total * factor + jnp.sum(weights, axis=0, keepdims=True)
        weighted = weighted * factor + jnp.sum(weights * slopes, axis=0, keepdims=True)
        inverse = 1.0 / total
        delta = weighted * inverse
        stats.append((factor * inverse, delta))
        prob = weights * inverse
        prob_b = prob.astype(jnp.bfloat16)
        slope_b = (prob * (slopes - delta)).astype(jnp.bfloat16)
        p_low[block, :span] = prob_b
        s_low[block, :span] = slope_b
        part_v = nn(prob_b, stacked(u_all, block, heads))
        part_k = nn(slope_b, stacked(q_all, block, heads))
        if block == 0:
            carry_k, carry_v = part_k[tok:], part_v[tok:]
            done_k, done_v = part_k[:tok], part_v[:tok]
        else:
            done_k, done_v = carry_k + part_k, carry_v + part_v
        g_back[block, 0] = done_k.astype(jnp.bfloat16)
        g_back[block, 1] = done_v.astype(jnp.bfloat16)
        copy = remote(
            g_back.at[block], g_in.at[core], g_send.at[block], g_recv.at[core], earlier * 2 + block
        )
        back.append(copy)
        pl.when(has_earlier)(copy.start)

    for block in range(2):
        span = (block + 1) * tok
        row = (2 - block) * tok
        scaled, delta = stats[block]
        prob = e_loc[block, :span] * scaled
        prob_b = prob.astype(jnp.bfloat16)
        slope_b = (prob * (d_loc[block, :span] - delta)).astype(jnp.bfloat16)
        p_low[block, row:] = prob_b
        s_low[block, row:] = slope_b
        part_v = nn(prob_b, stacked(u_all, block, heads))
        part_k = nn(slope_b, stacked(q_all, block, heads))
        if block == 0:
            carry_k, carry_v = part_k, part_v
        else:
            g_mine[0, 0] = carry_k + part_k[:tok]
            g_mine[0, 1] = carry_v + part_v[:tok]
            g_mine[1, 0] = part_k[tok:]
            g_mine[1, 1] = part_v[tok:]
    swap = remote(g_mine.at[peer], g_mate, gm_send, gm_recv, mate)
    swap.start()

    for block in range(2):
        keys = kv_all[block : block + 3, 0].reshape(3 * tok, HEAD)
        vals = kv_all[block : block + 3, 1].reshape(3 * tok, HEAD)
        out_t = nn(jnp.transpose(vals), p_low[block]).astype(jnp.bfloat16)
        gq_t = (nn(jnp.transpose(keys), s_low[block]) * scale).astype(jnp.bfloat16)
        for h in range(heads):
            cols = slice(h * HEAD, (h + 1) * HEAD)
            rows = slice(h * tok, (h + 1) * tok)
            out_buf[block, :, cols] = jnp.transpose(out_t[:, rows])
            gq_buf[block, :, cols] = jnp.transpose(gq_t[:, rows])
    outs = [
        remote(out_buf.at[peer], out_fin.at[core], o_send.at[0], o_recv.at[0], mate),
        remote(gq_buf.at[peer], gq_fin.at[core], o_send.at[1], o_recv.at[1], mate),
    ]
    stores = [
        pltpu.make_async_copy(out_buf.at[core], out_fin.at[core], store_sem.at[0]),
        pltpu.make_async_copy(gq_buf.at[core], gq_fin.at[core], store_sem.at[1]),
    ]
    for copy in outs + stores:
        copy.start()

    swap.wait_recv()
    for copy in (
        remote(out_buf.at[core], out_fin.at[peer], o_send.at[0], o_recv.at[0], mate),
        remote(gq_buf.at[core], gq_fin.at[peer], o_send.at[1], o_recv.at[1], mate),
    ):
        copy.wait_recv()
    for copy in stores:
        copy.wait()
    for copy in mate_out + outs + [swap]:
        copy.wait_send()

    @pl.when(has_later)
    def _():
        for copy in kv_out:
            copy.wait_send()

    @pl.when(has_earlier)
    def _():
        for copy in back:
            copy.wait_send()

    @pl.when(has_later)
    def _():
        for pack in range(2):
            remote(
                g_back.at[pack], g_in.at[pack], g_send.at[pack], g_recv.at[pack], mate
            ).wait_recv()

    mine = g_mine[pl.ds(core, 1)][0]
    for pack in range(2):
        own = core == pack
        sum_k = jnp.where(own, mine[0], g_mate[0]) + g_in[pack, 0].astype(jnp.float32)
        sum_v = jnp.where(own, mine[1], g_mate[1]) + g_in[pack, 1].astype(jnp.float32)
        gk_fin[pack] = (sum_k * scale).astype(jnp.bfloat16)
        gv_fin[pack] = sum_v.astype(jnp.bfloat16)


def store(*refs):
    count = (len(refs) - 1) // 2
    copies = [
        pltpu.make_async_copy(refs[i], refs[count + i], refs[-1].at[i]) for i in range(count)
    ]
    for copy in copies:
        copy.start()
    for copy in copies:
        copy.wait()


def per_device(queries, keys, values, upstream, doc_ids):
    packs, tok, features = queries.shape
    heads = features // HEAD
    bf16, f32 = jnp.bfloat16, jnp.float32
    wide = heads * tok
    dma = pltpu.SemaphoreType.DMA
    anywhere = pl.BlockSpec(memory_space=pl.ANY)
    shapes = (queries.shape, queries.shape, keys.shape, keys.shape)
    results = pl.pallas_call(
        kernel,
        out_shape=tuple(pltpu.VMEM(shape, bf16) for shape in shapes),
        in_specs=[anywhere] * 5,
        out_specs=(pl.BlockSpec(memory_space=pltpu.VMEM),) * 4,
        scratch_shapes=[
            pltpu.VMEM((2, tok, features), bf16),
            pltpu.VMEM((2, tok, features), bf16),
            pltpu.VMEM((4, 2, tok, HEAD), bf16),
            pltpu.VMEM((2, 2, tok, HEAD), bf16),
            pltpu.VMEM((2, 4 * tok), jnp.int32),
            pltpu.VMEM((2, 3 * tok, tok), f32),
            pltpu.VMEM((2, 2 * tok, wide), f32),
            pltpu.VMEM((2, 2 * tok, wide), f32),
            pltpu.VMEM((2, 3 * tok, wide), bf16),
            pltpu.VMEM((2, 3 * tok, wide), bf16),
            pltpu.VMEM((2, 2, tok, HEAD), bf16),
            pltpu.VMEM((2, 2, tok, HEAD), bf16),
            pltpu.VMEM((2, 2, tok, HEAD), f32),
            pltpu.VMEM((2, tok, HEAD), f32),
            pltpu.VMEM((2, tok, features), bf16),
            pltpu.VMEM((2, tok, features), bf16),
            dma((8,)),
            dma((2,)),
            dma((2,)),
            dma((3,)),
            dma((3,)),
            dma((2,)),
            dma((2,)),
            dma(()),
            dma(()),
            dma((2,)),
            dma((2,)),
            dma((2,)),
        ],
        compiler_params=pltpu.CompilerParams(
            collective_id=0, has_side_effects=True, vmem_limit_bytes=60 * 1024 * 1024
        ),
        name="attention_both_ways",
    )(queries, keys, values, upstream, doc_ids)
    return pl.pallas_call(
        store,
        out_shape=tuple(jax.ShapeDtypeStruct(shape, bf16) for shape in shapes),
        in_specs=[anywhere] * 4,
        out_specs=(anywhere,) * 4,
        scratch_shapes=[dma((4,))],
        compiler_params=pltpu.CompilerParams(vmem_limit_bytes=4 * 1024 * 1024),
        name="store_results",
    )(*results)


def solution(mesh):
    return jax.shard_map(
        per_device,
        mesh=mesh,
        in_specs=(P("dp", "ctx", None),) * 4 + (P("dp", None),),
        out_specs=(P("dp", "ctx", None),) * 4,
        check_vma=False,
    )
```

```python
import math

import jax
import jax.numpy as jnp
from jax import lax
from jax.experimental import pallas as pl
from jax.experimental.pallas import tpu as pltpu
from jax.sharding import PartitionSpec as P

MESH = pl.DeviceIdType.MESH
NEG_LARGE = -1e30
HEAD = 128


def nt(a, b):
    return lax.dot_general(a, b, (((1,), (1,)), ((), ())), preferred_element_type=jnp.float32)


def nn(a, b):
    return lax.dot_general(a, b, (((1,), (0,)), ((), ())), preferred_element_type=jnp.float32)


def kernel(
    q_hbm, k_hbm, v_hbm, u_hbm, ids_hbm,
    out_fin, gq_fin, gk_fin, gv_fin,
    q_all, u_all, kv_all, kv_own, ids_v, bias, stats, norms,
    e_loc, d_loc, p_low, s_low,
    g_back, g_in, g_mine, g_mate, out_buf, gq_buf,
    load_sem, kv_send, kv_recv, mate_send, mate_recv, pass_send, pass_recv,
    g_send, g_recv, gm_send, gm_recv, o_send, o_recv, store_sem,
):
    tok = q_all.shape[2]
    heads = q_all.shape[3] // HEAD
    scale = HEAD**-0.5
    log2_scale = scale * math.log2(math.e)
    ctx = lax.axis_index("ctx")
    dp = lax.axis_index("dp")
    chips = lax.axis_size("ctx") // 2
    chip = ctx // 2
    core = ctx % 2
    peer = 1 - core
    mate = chip * 2 + peer
    has_later = chip < chips - 1
    has_earlier = chip > 0
    later = lax.rem(chip + 1, chips)
    earlier = lax.rem(chip + chips - 1, chips)

    def remote(src, dst, send, recv, target):
        return pltpu.make_async_remote_copy(
            src_ref=src, dst_ref=dst, send_sem=send, recv_sem=recv,
            device_id=(dp, target), device_id_type=MESH,
        )

    barrier = pltpu.get_barrier_semaphore()

    @pl.when(has_earlier & (core == 1))
    def _():
        for target in (earlier * 2 + 1, earlier * 2):
            pl.semaphore_signal(barrier, inc=1, device_id=(dp, target), device_id_type=MESH)

    pl.semaphore_signal(barrier, inc=1, device_id=(dp, mate), device_id_type=MESH)

    ids_first = pl.multiple_of(earlier * 2 * tok, 2 * tok)
    ids_own = pl.multiple_of(chip * 2 * tok, 2 * tok)
    pairs = [
        (k_hbm, kv_own.at[:, 0]),
        (v_hbm, kv_own.at[:, 1]),
        (ids_hbm.at[:, pl.ds(ids_first, 2 * tok)], ids_v.at[:, pl.ds(0, 2 * tok)]),
        (ids_hbm.at[:, pl.ds(ids_own, 2 * tok)], ids_v.at[:, pl.ds(2 * tok, 2 * tok)]),
        (q_hbm, q_all.at[:, core]),
        (u_hbm, u_all.at[:, core]),
        (k_hbm, kv_all.at[:, 2 + core, 0]),
        (v_hbm, kv_all.at[:, 2 + core, 1]),
    ]
    loads = [
        pltpu.make_async_copy(src, dst, load_sem.at[i]) for i, (src, dst) in enumerate(pairs)
    ]
    for copy in loads:
        copy.start()

    @pl.when(jnp.logical_not(has_earlier))
    def _():
        for pack in range(2):
            kv_all[pack, 0:2] = jnp.zeros((2,) + kv_all.shape[2:], kv_all.dtype)

    @pl.when(jnp.logical_not(has_later))
    def _():
        g_in[...] = jnp.zeros(g_in.shape, g_in.dtype)

    for copy in loads[:2]:
        copy.wait()
    pl.semaphore_wait(barrier, jnp.where(has_later, 2, 1))

    kv_out = [
        remote(
            kv_own.at[pack], kv_all.at[pack, core], kv_send.at[pack], kv_recv.at[pack, core],
            later * 2 + 1,
        )
        for pack in range(2)
    ]

    @pl.when(has_later)
    def _():
        for copy in kv_out:
            copy.start()

    def mates(pack, block):
        return [
            remote(src.at[pack], dst, mate_send.at[pack, i], mate_recv.at[pack, i], mate)
            for i, (src, dst) in enumerate(
                (
                    (kv_own, kv_all.at[pack, 2 + block]),
                    (q_hbm, q_all.at[pack, block]),
                    (u_hbm, u_all.at[pack, block]),
                )
            )
        ]

    mate_out = [mates(0, core), mates(1, 0)]
    for copy in mate_out[0]:
        copy.start()

    @pl.when(core == 0)
    def _():
        for copy in mate_out[1]:
            copy.start()

    for copy in loads[2:4]:
        copy.wait()
    ids_two = ids_v[...]
    for pack in range(2):
        ids_row = ids_two[pack : pack + 1]
        lane = lax.broadcasted_iota(jnp.int32, ids_row.shape, 1)
        ids_row = jnp.where((lane < 2 * tok) & (chip == 0), -1, ids_row)
        ids_col = jnp.transpose(jnp.broadcast_to(ids_row, (tok, 4 * tok)))
        for block in range(2):
            first = block * tok
            q_first = (2 + block) * tok
            key_pos = first + lax.broadcasted_iota(jnp.int32, (3 * tok, tok), 0)
            query_pos = q_first + lax.broadcasted_iota(jnp.int32, (3 * tok, tok), 1)
            allowed = (ids_col[first : first + 3 * tok] == ids_row[:, q_first : q_first + tok]) & (
                key_pos <= query_pos
            )
            bias[pack, block] = jnp.where(allowed, 0.0, NEG_LARGE)

    def stacked(ref, pack, block):
        return jnp.concatenate(
            [ref[pack, block, :, h * HEAD : (h + 1) * HEAD] for h in range(heads)], axis=0
        )

    def tile(pack, block, key_first, key_blocks):
        span = key_blocks * tok
        keys = kv_all[pack, key_first : key_first + key_blocks, 0].reshape(span, HEAD)
        vals = kv_all[pack, key_first : key_first + key_blocks, 1].reshape(span, HEAD)
        row = (key_first - block) * tok
        add = bias[pack, block, row : row + span]
        scores = nt(keys, stacked(q_all, pack, block))
        slopes = nt(vals, stacked(u_all, pack, block))
        scores = scores * log2_scale + jnp.concatenate([add] * heads, axis=1)
        return scores, slopes

    def local_part(pack, keep):
        for block in range(2):
            span = (block + 1) * tok
            scores, slopes = tile(pack, block, 2, block + 1)
            peak = jnp.max(scores, axis=0, keepdims=True)
            weights = jnp.exp2(scores - peak)
            if keep:
                e_loc[block, :span] = weights
                d_loc[block, :span] = slopes
            stats[pack, block, 0:1] = peak
            stats[pack, block, 1:2] = jnp.sum(weights, axis=0, keepdims=True)
            stats[pack, block, 2:3] = jnp.sum(weights * slopes, axis=0, keepdims=True)

    def back_copy(pack, block):
        return remote(
            g_back.at[pack, block], g_in.at[pack], g_send.at[pack, block], g_recv.at[pack],
            earlier * 2 + block,
        )

    def boundary_part(pack, keep, send):
        for block in range(2):
            span = (2 - block) * tok
            scores, slopes = tile(pack, block, block, 2 - block)
            peak = stats[pack, block, 0:1]
            new_peak = jnp.maximum(peak, jnp.max(scores, axis=0, keepdims=True))
            factor = jnp.exp2(peak - new_peak)
            weights = jnp.exp2(scores - new_peak)
            total = stats[pack, block, 1:2] * factor + jnp.sum(weights, axis=0, keepdims=True)
            weighted = stats[pack, block, 2:3] * factor + jnp.sum(
                weights * slopes, axis=0, keepdims=True
            )
            inverse = 1.0 / total
            delta = weighted * inverse
            prob = weights * inverse
            prob_b = prob.astype(jnp.bfloat16)
            slope_b = (prob * (slopes - delta)).astype(jnp.bfloat16)
            if keep:
                norms[block, 0:1] = factor * inverse
                norms[block, 1:2] = delta
                p_low[block, :span] = prob_b
                s_low[block, :span] = slope_b
            if send:
                part_v = nn(prob_b, stacked(u_all, pack, block))
                part_k = nn(slope_b, stacked(q_all, pack, block))
                if block == 0:
                    carry_k, carry_v = part_k[tok:], part_v[tok:]
                    done_k, done_v = part_k[:tok], part_v[:tok]
                else:
                    done_k, done_v = carry_k + part_k, carry_v + part_v
                g_back[pack, block, 0] = done_k.astype(jnp.bfloat16)
                g_back[pack, block, 1] = done_v.astype(jnp.bfloat16)
                pl.when(has_earlier)(back_copy(pack, block).start)

    def kv_in(pack):
        for block in range(2):
            remote(
                kv_own.at[0], kv_all.at[pack, block], kv_send.at[0], kv_recv.at[pack, block], mate
            ).wait_recv()

    passed = remote(kv_all.at[0, pl.ds(0, 2)], kv_all.at[0, pl.ds(0, 2)], pass_send, pass_recv, mate)

    for copy in loads[4:]:
        copy.wait()
    for copy in mates(0, peer):
        copy.wait_recv()

    @pl.when(core == 0)
    def _():
        local_part(0, True)
        pl.when(has_earlier)(passed.wait_recv)
        boundary_part(0, True, False)

    @pl.when(core == 1)
    def _():
        local_part(0, False)
        for copy in mates(1, 0):
            copy.wait_recv()
        local_part(1, True)

        @pl.when(has_earlier)
        def _():
            kv_in(0)
            passed.start()

        boundary_part(0, False, True)

        @pl.when(has_earlier)
        def _():
            kv_in(1)

        boundary_part(1, True, True)

    for block in range(2):
        span = (block + 1) * tok
        row = (2 - block) * tok
        prob = e_loc[block, :span] * norms[block, 0:1]
        prob_b = prob.astype(jnp.bfloat16)
        slope_b = (prob * (d_loc[block, :span] - norms[block, 1:2])).astype(jnp.bfloat16)
        p_low[block, row:] = prob_b
        s_low[block, row:] = slope_b
        part_v = nn(prob_b, stacked(u_all, core, block))
        part_k = nn(slope_b, stacked(q_all, core, block))
        if block == 0:
            carry_k, carry_v = part_k, part_v
        else:
            g_mine[0, 0] = carry_k + part_k[:tok]
            g_mine[0, 1] = carry_v + part_v[:tok]
            g_mine[1, 0] = part_k[tok:]
            g_mine[1, 1] = part_v[tok:]
    swap = remote(g_mine.at[peer], g_mate, gm_send, gm_recv, mate)
    swap.start()

    for block in range(2):
        keys = kv_all[core, block : block + 3, 0].reshape(3 * tok, HEAD)
        vals = kv_all[core, block : block + 3, 1].reshape(3 * tok, HEAD)
        out_t = nn(jnp.transpose(vals), p_low[block]).astype(jnp.bfloat16)
        gq_t = (nn(jnp.transpose(keys), s_low[block]) * scale).astype(jnp.bfloat16)
        for h in range(heads):
            cols = slice(h * HEAD, (h + 1) * HEAD)
            rows = slice(h * tok, (h + 1) * tok)
            out_buf[block, :, cols] = jnp.transpose(out_t[:, rows])
            gq_buf[block, :, cols] = jnp.transpose(gq_t[:, rows])
    outs = [
        remote(out_buf.at[peer], out_fin.at[core], o_send.at[0], o_recv.at[0], mate),
        remote(gq_buf.at[peer], gq_fin.at[core], o_send.at[1], o_recv.at[1], mate),
    ]
    stores = [
        pltpu.make_async_copy(out_buf.at[core], out_fin.at[core], store_sem.at[0]),
        pltpu.make_async_copy(gq_buf.at[core], gq_fin.at[core], store_sem.at[1]),
    ]
    for copy in outs + stores:
        copy.start()

    swap.wait_recv()
    for copy in (
        remote(out_buf.at[core], out_fin.at[peer], o_send.at[0], o_recv.at[0], mate),
        remote(gq_buf.at[core], gq_fin.at[peer], o_send.at[1], o_recv.at[1], mate),
    ):
        copy.wait_recv()
    for copy in stores:
        copy.wait()
    for copy in mate_out[0] + outs + [swap]:
        copy.wait_send()

    @pl.when(core == 0)
    def _():
        for copy in mate_out[1]:
            copy.wait_send()

    @pl.when(has_later)
    def _():
        for copy in kv_out:
            copy.wait_send()

    @pl.when(has_earlier & (core == 1))
    def _():
        passed.wait_send()
        for pack in range(2):
            for block in range(2):
                back_copy(pack, block).wait_send()

    @pl.when(has_later)
    def _():
        for pack in range(2):
            remote(
                g_back.at[pack, 0], g_in.at[pack], g_send.at[pack, 0], g_recv.at[pack], mate
            ).wait_recv()

    mine = g_mine[pl.ds(core, 1)][0]
    for pack in range(2):
        own = core == pack
        sum_k = jnp.where(own, mine[0], g_mate[0]) + g_in[pack, 0].astype(jnp.float32)
        sum_v = jnp.where(own, mine[1], g_mate[1]) + g_in[pack, 1].astype(jnp.float32)
        gk_fin[pack] = (sum_k * scale).astype(jnp.bfloat16)
        gv_fin[pack] = sum_v.astype(jnp.bfloat16)


def store(*refs):
    count = (len(refs) - 1) // 2
    copies = [
        pltpu.make_async_copy(refs[i], refs[count + i], refs[-1].at[i]) for i in range(count)
    ]
    for copy in copies:
        copy.start()
    for copy in copies:
        copy.wait()


def per_device(queries, keys, values, upstream, doc_ids):
    packs, tok, features = queries.shape
    heads = features // HEAD
    bf16, f32 = jnp.bfloat16, jnp.float32
    wide = heads * tok
    dma = pltpu.SemaphoreType.DMA
    anywhere = pl.BlockSpec(memory_space=pl.ANY)
    shapes = (queries.shape, queries.shape, keys.shape, keys.shape)
    results = pl.pallas_call(
        kernel,
        out_shape=tuple(pltpu.VMEM(shape, bf16) for shape in shapes),
        in_specs=[anywhere] * 5,
        out_specs=(pl.BlockSpec(memory_space=pltpu.VMEM),) * 4,
        scratch_shapes=[
            pltpu.VMEM((2, 2, tok, features), bf16),
            pltpu.VMEM((2, 2, tok, features), bf16),
            pltpu.VMEM((2, 4, 2, tok, HEAD), bf16),
            pltpu.VMEM((2, 2, tok, HEAD), bf16),
            pltpu.VMEM((2, 4 * tok), jnp.int32),
            pltpu.VMEM((2, 2, 3 * tok, tok), f32),
            pltpu.VMEM((2, 2, 8, wide), f32),
            pltpu.VMEM((2, 8, wide), f32),
            pltpu.VMEM((2, 2 * tok, wide), f32),
            pltpu.VMEM((2, 2 * tok, wide), f32),
            pltpu.VMEM((2, 3 * tok, wide), bf16),
            pltpu.VMEM((2, 3 * tok, wide), bf16),
            pltpu.VMEM((2, 2, 2, tok, HEAD), bf16),
            pltpu.VMEM((2, 2, tok, HEAD), bf16),
            pltpu.VMEM((2, 2, tok, HEAD), f32),
            pltpu.VMEM((2, tok, HEAD), f32),
            pltpu.VMEM((2, tok, features), bf16),
            pltpu.VMEM((2, tok, features), bf16),
            dma((8,)),
            dma((2,)),
            dma((2, 2)),
            dma((2, 3)),
            dma((2, 3)),
            dma(()),
            dma(()),
            dma((2, 2)),
            dma((2,)),
            dma(()),
            dma(()),
            dma((2,)),
            dma((2,)),
            dma((2,)),
        ],
        compiler_params=pltpu.CompilerParams(
            collective_id=0, has_side_effects=True, vmem_limit_bytes=60 * 1024 * 1024
        ),
        name="attention_both_ways",
    )(queries, keys, values, upstream, doc_ids)
    return pl.pallas_call(
        store,
        out_shape=tuple(jax.ShapeDtypeStruct(shape, bf16) for shape in shapes),
        in_specs=[anywhere] * 4,
        out_specs=(anywhere,) * 4,
        scratch_shapes=[dma((4,))],
        compiler_params=pltpu.CompilerParams(vmem_limit_bytes=4 * 1024 * 1024),
        name="store_results",
    )(*results)


def solution(mesh):
    return jax.shard_map(
        per_device,
        mesh=mesh,
        in_specs=(P("dp", "ctx", None),) * 4 + (P("dp", None),),
        out_specs=(P("dp", "ctx", None),) * 4,
        check_vma=False,
    )
```

```python
import math

import jax
import jax.numpy as jnp
from jax import lax
from jax.experimental import pallas as pl
from jax.experimental.pallas import tpu as pltpu
from jax.sharding import PartitionSpec as P

MESH = pl.DeviceIdType.MESH
NEG_LARGE = -1e30
HEAD = 128


def nt(a, b):
    return lax.dot_general(a, b, (((1,), (1,)), ((), ())), preferred_element_type=jnp.float32)


def nn(a, b):
    return lax.dot_general(a, b, (((1,), (0,)), ((), ())), preferred_element_type=jnp.float32)


def kernel(
    q_hbm, k_hbm, v_hbm, u_hbm, ids_hbm,
    out_fin, gq_fin, gk_fin, gv_fin,
    q_all, u_all, kv_all, kv_own, ids_v, bias, stats, norms,
    e_loc, d_loc, p_low, s_low,
    g_back, g_in, g_mine, g_mate, out_buf, gq_buf,
    load_sem, kv_send, kv_recv, mate_send, mate_recv, pass_send, pass_recv,
    g_send, g_recv, gm_send, gm_recv, o_send, o_recv, store_sem,
):
    tok = q_all.shape[2]
    heads = q_all.shape[3] // HEAD
    scale = HEAD**-0.5
    log2_scale = scale * math.log2(math.e)
    ctx = lax.axis_index("ctx")
    dp = lax.axis_index("dp")
    chips = lax.axis_size("ctx") // 2
    chip = ctx // 2
    core = ctx % 2
    peer = 1 - core
    mate = chip * 2 + peer
    has_later = chip < chips - 1
    has_earlier = chip > 0
    later = lax.rem(chip + 1, chips)
    earlier = lax.rem(chip + chips - 1, chips)

    def remote(src, dst, send, recv, target):
        return pltpu.make_async_remote_copy(
            src_ref=src, dst_ref=dst, send_sem=send, recv_sem=recv,
            device_id=(dp, target), device_id_type=MESH,
        )

    barrier = pltpu.get_barrier_semaphore()

    @pl.when(has_earlier & (core == 1))
    def _():
        for target in (earlier * 2 + 1, earlier * 2):
            pl.semaphore_signal(barrier, inc=1, device_id=(dp, target), device_id_type=MESH)

    pl.semaphore_signal(barrier, inc=1, device_id=(dp, mate), device_id_type=MESH)

    ids_first = pl.multiple_of(earlier * 2 * tok, 2 * tok)
    ids_own = pl.multiple_of(chip * 2 * tok, 2 * tok)
    pairs = [
        (k_hbm, kv_own.at[:, 0]),
        (v_hbm, kv_own.at[:, 1]),
        (ids_hbm.at[:, pl.ds(ids_first, 2 * tok)], ids_v.at[:, pl.ds(0, 2 * tok)]),
        (ids_hbm.at[:, pl.ds(ids_own, 2 * tok)], ids_v.at[:, pl.ds(2 * tok, 2 * tok)]),
        (q_hbm, q_all.at[:, core]),
        (u_hbm, u_all.at[:, core]),
        (k_hbm, kv_all.at[:, 2 + core, 0]),
        (v_hbm, kv_all.at[:, 2 + core, 1]),
    ]
    loads = [
        pltpu.make_async_copy(src, dst, load_sem.at[i]) for i, (src, dst) in enumerate(pairs)
    ]
    for copy in loads:
        copy.start()

    @pl.when(jnp.logical_not(has_earlier))
    def _():
        for pack in range(2):
            kv_all[pack, 0:2] = jnp.zeros((2,) + kv_all.shape[2:], kv_all.dtype)

    @pl.when(jnp.logical_not(has_later))
    def _():
        g_in[...] = jnp.zeros(g_in.shape, g_in.dtype)

    for copy in loads[:2]:
        copy.wait()
    pl.semaphore_wait(barrier, jnp.where(has_later, 2, 1))

    kv_out = [
        remote(
            kv_own.at[pack], kv_all.at[pack, core], kv_send.at[pack], kv_recv.at[pack, core],
            later * 2 + 1,
        )
        for pack in range(2)
    ]

    @pl.when(has_later)
    def _():
        kv_out[0].start()

    def mates(pack, block):
        return [
            remote(src.at[pack], dst, mate_send.at[pack, i], mate_recv.at[pack, i], mate)
            for i, (src, dst) in enumerate(
                (
                    (kv_own, kv_all.at[pack, 2 + block]),
                    (q_hbm, q_all.at[pack, block]),
                    (u_hbm, u_all.at[pack, block]),
                )
            )
        ]

    mate_out = [mates(0, core), mates(1, 0)]
    for copy in mate_out[0]:
        copy.start()

    @pl.when(core == 0)
    def _():
        for copy in mate_out[1]:
            copy.start()

    @pl.when(has_later & (core == 0))
    def _():
        kv_out[1].start()

    for copy in loads[2:4]:
        copy.wait()
    ids_two = ids_v[...]
    for pack in range(2):
        ids_row = ids_two[pack : pack + 1]
        lane = lax.broadcasted_iota(jnp.int32, ids_row.shape, 1)
        ids_row = jnp.where((lane < 2 * tok) & (chip == 0), -1, ids_row)
        ids_col = jnp.transpose(jnp.broadcast_to(ids_row, (tok, 4 * tok)))
        for block in range(2):
            first = block * tok
            q_first = (2 + block) * tok
            key_pos = first + lax.broadcasted_iota(jnp.int32, (3 * tok, tok), 0)
            query_pos = q_first + lax.broadcasted_iota(jnp.int32, (3 * tok, tok), 1)
            allowed = (ids_col[first : first + 3 * tok] == ids_row[:, q_first : q_first + tok]) & (
                key_pos <= query_pos
            )
            bias[pack, block] = jnp.where(allowed, 0.0, NEG_LARGE)

    def stacked(ref, pack, block):
        return jnp.concatenate(
            [ref[pack, block, :, h * HEAD : (h + 1) * HEAD] for h in range(heads)], axis=0
        )

    def tile(pack, block, key_first, key_blocks):
        span = key_blocks * tok
        keys = kv_all[pack, key_first : key_first + key_blocks, 0].reshape(span, HEAD)
        vals = kv_all[pack, key_first : key_first + key_blocks, 1].reshape(span, HEAD)
        row = (key_first - block) * tok
        add = bias[pack, block, row : row + span]
        scores = nt(keys, stacked(q_all, pack, block))
        slopes = nt(vals, stacked(u_all, pack, block))
        scores = scores * log2_scale + jnp.concatenate([add] * heads, axis=1)
        return scores, slopes

    def local_part(pack, keep):
        for block in range(2):
            span = (block + 1) * tok
            scores, slopes = tile(pack, block, 2, block + 1)
            peak = jnp.max(scores, axis=0, keepdims=True)
            weights = jnp.exp2(scores - peak)
            if keep:
                e_loc[block, :span] = weights
                d_loc[block, :span] = slopes
            stats[pack, block, 0:1] = peak
            stats[pack, block, 1:2] = jnp.sum(weights, axis=0, keepdims=True)
            stats[pack, block, 2:3] = jnp.sum(weights * slopes, axis=0, keepdims=True)

    def back_copy(pack, block):
        return remote(
            g_back.at[pack, block], g_in.at[pack], g_send.at[pack, block], g_recv.at[pack],
            earlier * 2 + block,
        )

    def boundary_part(pack, keep, send):
        for block in range(2):
            span = (2 - block) * tok
            scores, slopes = tile(pack, block, block, 2 - block)
            peak = stats[pack, block, 0:1]
            new_peak = jnp.maximum(peak, jnp.max(scores, axis=0, keepdims=True))
            factor = jnp.exp2(peak - new_peak)
            weights = jnp.exp2(scores - new_peak)
            total = stats[pack, block, 1:2] * factor + jnp.sum(weights, axis=0, keepdims=True)
            weighted = stats[pack, block, 2:3] * factor + jnp.sum(
                weights * slopes, axis=0, keepdims=True
            )
            inverse = 1.0 / total
            delta = weighted * inverse
            prob = weights * inverse
            prob_b = prob.astype(jnp.bfloat16)
            slope_b = (prob * (slopes - delta)).astype(jnp.bfloat16)
            if keep:
                norms[block, 0:1] = factor * inverse
                norms[block, 1:2] = delta
                p_low[block, :span] = prob_b
                s_low[block, :span] = slope_b
            if send:
                part_v = nn(prob_b, stacked(u_all, pack, block))
                part_k = nn(slope_b, stacked(q_all, pack, block))
                if block == 0:
                    carry_k, carry_v = part_k[tok:], part_v[tok:]
                    done_k, done_v = part_k[:tok], part_v[:tok]
                else:
                    done_k, done_v = carry_k + part_k, carry_v + part_v
                g_back[pack, block, 0] = done_k.astype(jnp.bfloat16)
                g_back[pack, block, 1] = done_v.astype(jnp.bfloat16)
                back_copy(pack, block).start()

    def no_boundary(pack):
        for block in range(2):
            inverse = 1.0 / stats[pack, block, 1:2]
            norms[block, 0:1] = inverse
            norms[block, 1:2] = stats[pack, block, 2:3] * inverse
            span = (2 - block) * tok
            p_low[block, :span] = jnp.zeros((span, heads * tok), jnp.bfloat16)
            s_low[block, :span] = jnp.zeros((span, heads * tok), jnp.bfloat16)

    def kv_in(pack):
        for block in range(2):
            remote(
                kv_own.at[0], kv_all.at[pack, block], kv_send.at[0], kv_recv.at[pack, block], mate
            ).wait_recv()

    passed = remote(kv_all.at[0, pl.ds(0, 2)], kv_all.at[0, pl.ds(0, 2)], pass_send, pass_recv, mate)

    for copy in loads[4:]:
        copy.wait()
    for copy in mates(0, peer):
        copy.wait_recv()

    @pl.when(has_later & (core == 1))
    def _():
        kv_out[1].start()


    @pl.when(core == 0)
    def _():
        local_part(0, True)

        @pl.when(has_earlier)
        def _():
            passed.wait_recv()
            boundary_part(0, True, False)

    @pl.when(core == 1)
    def _():
        local_part(0, False)
        for copy in mates(1, 0):
            copy.wait_recv()
        local_part(1, True)

        @pl.when(has_earlier)
        def _():
            kv_in(0)
            passed.start()
            boundary_part(0, False, True)
            kv_in(1)
            boundary_part(1, True, True)

    @pl.when(jnp.logical_not(has_earlier))
    def _():
        no_boundary(core)

    for block in range(2):
        span = (block + 1) * tok
        row = (2 - block) * tok
        prob = e_loc[block, :span] * norms[block, 0:1]
        prob_b = prob.astype(jnp.bfloat16)
        slope_b = (prob * (d_loc[block, :span] - norms[block, 1:2])).astype(jnp.bfloat16)
        p_low[block, row:] = prob_b
        s_low[block, row:] = slope_b
        part_v = nn(prob_b, stacked(u_all, core, block))
        part_k = nn(slope_b, stacked(q_all, core, block))
        if block == 0:
            carry_k, carry_v = part_k, part_v
        else:
            g_mine[0, 0] = carry_k + part_k[:tok]
            g_mine[0, 1] = carry_v + part_v[:tok]
            g_mine[1, 0] = part_k[tok:]
            g_mine[1, 1] = part_v[tok:]
    swap = remote(g_mine.at[peer], g_mate, gm_send, gm_recv, mate)
    swap.start()

    for block in range(2):
        keys = kv_all[core, block : block + 3, 0].reshape(3 * tok, HEAD)
        vals = kv_all[core, block : block + 3, 1].reshape(3 * tok, HEAD)
        out_t = nn(jnp.transpose(vals), p_low[block]).astype(jnp.bfloat16)
        gq_t = (nn(jnp.transpose(keys), s_low[block]) * scale).astype(jnp.bfloat16)
        for h in range(heads):
            cols = slice(h * HEAD, (h + 1) * HEAD)
            rows = slice(h * tok, (h + 1) * tok)
            out_buf[block, :, cols] = jnp.transpose(out_t[:, rows])
            gq_buf[block, :, cols] = jnp.transpose(gq_t[:, rows])
    outs = [
        remote(out_buf.at[peer], out_fin.at[core], o_send.at[0], o_recv.at[0], mate),
        remote(gq_buf.at[peer], gq_fin.at[core], o_send.at[1], o_recv.at[1], mate),
    ]
    stores = [
        pltpu.make_async_copy(out_buf.at[core], out_fin.at[core], store_sem.at[0]),
        pltpu.make_async_copy(gq_buf.at[core], gq_fin.at[core], store_sem.at[1]),
    ]
    for copy in outs + stores:
        copy.start()

    swap.wait_recv()
    for copy in (
        remote(out_buf.at[core], out_fin.at[peer], o_send.at[0], o_recv.at[0], mate),
        remote(gq_buf.at[core], gq_fin.at[peer], o_send.at[1], o_recv.at[1], mate),
    ):
        copy.wait_recv()
    for copy in stores:
        copy.wait()
    for copy in mate_out[0] + outs + [swap]:
        copy.wait_send()

    @pl.when(core == 0)
    def _():
        for copy in mate_out[1]:
            copy.wait_send()

    @pl.when(has_later)
    def _():
        for copy in kv_out:
            copy.wait_send()

    @pl.when(has_earlier & (core == 1))
    def _():
        passed.wait_send()
        for pack in range(2):
            for block in range(2):
                back_copy(pack, block).wait_send()

    @pl.when(has_later)
    def _():
        for pack in range(2):
            remote(
                g_back.at[pack, 0], g_in.at[pack], g_send.at[pack, 0], g_recv.at[pack], mate
            ).wait_recv()

    mine = g_mine[pl.ds(core, 1)][0]
    for pack in range(2):
        own = core == pack
        sum_k = jnp.where(own, mine[0], g_mate[0]) + g_in[pack, 0].astype(jnp.float32)
        sum_v = jnp.where(own, mine[1], g_mate[1]) + g_in[pack, 1].astype(jnp.float32)
        gk_fin[pack] = (sum_k * scale).astype(jnp.bfloat16)
        gv_fin[pack] = sum_v.astype(jnp.bfloat16)


def store(*refs):
    count = (len(refs) - 1) // 2
    copies = [
        pltpu.make_async_copy(refs[i], refs[count + i], refs[-1].at[i]) for i in range(count)
    ]
    for copy in copies:
        copy.start()
    for copy in copies:
        copy.wait()


def per_device(queries, keys, values, upstream, doc_ids):
    packs, tok, features = queries.shape
    heads = features // HEAD
    bf16, f32 = jnp.bfloat16, jnp.float32
    wide = heads * tok
    dma = pltpu.SemaphoreType.DMA
    anywhere = pl.BlockSpec(memory_space=pl.ANY)
    shapes = (queries.shape, queries.shape, keys.shape, keys.shape)
    results = pl.pallas_call(
        kernel,
        out_shape=tuple(pltpu.VMEM(shape, bf16) for shape in shapes),
        in_specs=[anywhere] * 5,
        out_specs=(pl.BlockSpec(memory_space=pltpu.VMEM),) * 4,
        scratch_shapes=[
            pltpu.VMEM((2, 2, tok, features), bf16),
            pltpu.VMEM((2, 2, tok, features), bf16),
            pltpu.VMEM((2, 4, 2, tok, HEAD), bf16),
            pltpu.VMEM((2, 2, tok, HEAD), bf16),
            pltpu.VMEM((2, 4 * tok), jnp.int32),
            pltpu.VMEM((2, 2, 3 * tok, tok), f32),
            pltpu.VMEM((2, 2, 8, wide), f32),
            pltpu.VMEM((2, 8, wide), f32),
            pltpu.VMEM((2, 2 * tok, wide), f32),
            pltpu.VMEM((2, 2 * tok, wide), f32),
            pltpu.VMEM((2, 3 * tok, wide), bf16),
            pltpu.VMEM((2, 3 * tok, wide), bf16),
            pltpu.VMEM((2, 2, 2, tok, HEAD), bf16),
            pltpu.VMEM((2, 2, tok, HEAD), bf16),
            pltpu.VMEM((2, 2, tok, HEAD), f32),
            pltpu.VMEM((2, tok, HEAD), f32),
            pltpu.VMEM((2, tok, features), bf16),
            pltpu.VMEM((2, tok, features), bf16),
            dma((8,)),
            dma((2,)),
            dma((2, 2)),
            dma((2, 3)),
            dma((2, 3)),
            dma(()),
            dma(()),
            dma((2, 2)),
            dma((2,)),
            dma(()),
            dma(()),
            dma((2,)),
            dma((2,)),
            dma((2,)),
        ],
        compiler_params=pltpu.CompilerParams(
            collective_id=0, has_side_effects=True, vmem_limit_bytes=60 * 1024 * 1024
        ),
        name="attention_both_ways",
    )(queries, keys, values, upstream, doc_ids)
    return pl.pallas_call(
        store,
        out_shape=tuple(jax.ShapeDtypeStruct(shape, bf16) for shape in shapes),
        in_specs=[anywhere] * 4,
        out_specs=(anywhere,) * 4,
        scratch_shapes=[dma((4,))],
        compiler_params=pltpu.CompilerParams(vmem_limit_bytes=4 * 1024 * 1024),
        name="store_results",
    )(*results)


def solution(mesh):
    return jax.shard_map(
        per_device,
        mesh=mesh,
        in_specs=(P("dp", "ctx", None),) * 4 + (P("dp", None),),
        out_specs=(P("dp", "ctx", None),) * 4,
        check_vma=False,
    )
```

```python
import math

import jax
import jax.numpy as jnp
from jax import lax
from jax.experimental import pallas as pl
from jax.experimental.pallas import tpu as pltpu
from jax.sharding import PartitionSpec as P

MESH = pl.DeviceIdType.MESH
NEG_LARGE = -1e30
HEAD = 128


def nt(a, b):
    return lax.dot_general(a, b, (((1,), (1,)), ((), ())), preferred_element_type=jnp.float32)


def nn(a, b):
    return lax.dot_general(a, b, (((1,), (0,)), ((), ())), preferred_element_type=jnp.float32)


def kernel(
    q_hbm, k_hbm, v_hbm, u_hbm, ids_hbm,
    out_fin, gq_fin, gk_fin, gv_fin,
    q_all, u_all, kv_all, kv_own, ids_v, bias, stats, norms,
    e_loc, d_loc, p_low, s_low,
    g_back, g_in, g_mine, g_mate, out_buf, gq_buf,
    load_sem, kv_send, kv_recv, mate_send, mate_recv, pass_send, pass_recv,
    g_send, g_recv, gm_send, gm_recv, o_send, o_recv, store_sem,
):
    tok = q_all.shape[2]
    heads = q_all.shape[3] // HEAD
    scale = HEAD**-0.5
    log2_scale = scale * math.log2(math.e)
    ctx = lax.axis_index("ctx")
    dp = lax.axis_index("dp")
    chips = lax.axis_size("ctx") // 2
    chip = ctx // 2
    core = ctx % 2
    peer = 1 - core
    mate = chip * 2 + peer
    has_later = chip < chips - 1
    has_earlier = chip > 0
    later = lax.rem(chip + 1, chips)
    earlier = lax.rem(chip + chips - 1, chips)

    def remote(src, dst, send, recv, target):
        return pltpu.make_async_remote_copy(
            src_ref=src, dst_ref=dst, send_sem=send, recv_sem=recv,
            device_id=(dp, target), device_id_type=MESH,
        )

    barrier = pltpu.get_barrier_semaphore()

    @pl.when(has_earlier & (core == 1))
    def _():
        for target in (earlier * 2 + 1, earlier * 2):
            pl.semaphore_signal(barrier, inc=1, device_id=(dp, target), device_id_type=MESH)

    pl.semaphore_signal(barrier, inc=1, device_id=(dp, mate), device_id_type=MESH)

    ids_first = pl.multiple_of(earlier * 2 * tok, 2 * tok)
    ids_own = pl.multiple_of(chip * 2 * tok, 2 * tok)
    pairs = [
        (k_hbm.at[0], kv_own.at[0, 0]),
        (v_hbm.at[0], kv_own.at[0, 1]),
        (k_hbm.at[1], kv_own.at[1, 0]),
        (v_hbm.at[1], kv_own.at[1, 1]),
        (ids_hbm.at[:, pl.ds(ids_first, 2 * tok)], ids_v.at[:, pl.ds(0, 2 * tok)]),
        (ids_hbm.at[:, pl.ds(ids_own, 2 * tok)], ids_v.at[:, pl.ds(2 * tok, 2 * tok)]),
        (q_hbm, q_all.at[:, core]),
        (u_hbm, u_all.at[:, core]),
        (k_hbm, kv_all.at[:, 2 + core, 0]),
        (v_hbm, kv_all.at[:, 2 + core, 1]),
    ]
    loads = [
        pltpu.make_async_copy(src, dst, load_sem.at[i]) for i, (src, dst) in enumerate(pairs)
    ]
    for copy in loads:
        copy.start()

    @pl.when(jnp.logical_not(has_earlier))
    def _():
        for pack in range(2):
            kv_all[pack, 0:2] = jnp.zeros((2,) + kv_all.shape[2:], kv_all.dtype)

    @pl.when(jnp.logical_not(has_later))
    def _():
        g_in[...] = jnp.zeros(g_in.shape, g_in.dtype)

    for copy in loads[:4]:
        copy.wait()
    pl.semaphore_wait(barrier, jnp.where(has_later, 2, 1))

    kv_out = [
        remote(
            kv_own.at[pack], kv_all.at[pack, core], kv_send.at[pack], kv_recv.at[pack, core],
            later * 2 + 1,
        )
        for pack in range(2)
    ]

    @pl.when(has_later)
    def _():
        kv_out[0].start()

    def mates(pack, block):
        return [
            remote(src.at[pack], dst, mate_send.at[pack, i], mate_recv.at[pack, i], mate)
            for i, (src, dst) in enumerate(
                (
                    (kv_own, kv_all.at[pack, 2 + block]),
                    (q_hbm, q_all.at[pack, block]),
                    (u_hbm, u_all.at[pack, block]),
                )
            )
        ]

    mate_out = [mates(0, core), mates(1, 0)]
    for copy in mate_out[0]:
        copy.start()

    @pl.when(core == 0)
    def _():
        for copy in mate_out[1]:
            copy.start()

    @pl.when(has_later & (core == 0))
    def _():
        kv_out[1].start()

    for copy in loads[4:6]:
        copy.wait()
    ids_two = ids_v[...]
    for pack in range(2):
        ids_row = ids_two[pack : pack + 1]
        lane = lax.broadcasted_iota(jnp.int32, ids_row.shape, 1)
        ids_row = jnp.where((lane < 2 * tok) & (chip == 0), -1, ids_row)
        ids_col = jnp.transpose(jnp.broadcast_to(ids_row, (tok, 4 * tok)))
        for block in range(2):
            first = block * tok
            q_first = (2 + block) * tok
            key_pos = first + lax.broadcasted_iota(jnp.int32, (3 * tok, tok), 0)
            query_pos = q_first + lax.broadcasted_iota(jnp.int32, (3 * tok, tok), 1)
            allowed = (ids_col[first : first + 3 * tok] == ids_row[:, q_first : q_first + tok]) & (
                key_pos <= query_pos
            )
            bias[pack, block] = jnp.where(allowed, 0.0, NEG_LARGE)

    def stacked(ref, pack, block):
        return jnp.concatenate(
            [ref[pack, block, :, h * HEAD : (h + 1) * HEAD] for h in range(heads)], axis=0
        )

    def tile(pack, block, key_first, key_blocks):
        span = key_blocks * tok
        keys = kv_all[pack, key_first : key_first + key_blocks, 0].reshape(span, HEAD)
        vals = kv_all[pack, key_first : key_first + key_blocks, 1].reshape(span, HEAD)
        row = (key_first - block) * tok
        add = bias[pack, block, row : row + span]
        scores = nt(keys, stacked(q_all, pack, block))
        slopes = nt(vals, stacked(u_all, pack, block))
        scores = scores * log2_scale + jnp.concatenate([add] * heads, axis=1)
        return scores, slopes

    def local_part(pack, keep):
        for block in range(2):
            span = (block + 1) * tok
            scores, slopes = tile(pack, block, 2, block + 1)
            peak = jnp.max(scores, axis=0, keepdims=True)
            weights = jnp.exp2(scores - peak)
            if keep:
                e_loc[block, :span] = weights
                d_loc[block, :span] = slopes
            stats[pack, block, 0:1] = peak
            stats[pack, block, 1:2] = jnp.sum(weights, axis=0, keepdims=True)
            stats[pack, block, 2:3] = jnp.sum(weights * slopes, axis=0, keepdims=True)

    def back_copy(pack, block):
        return remote(
            g_back.at[pack, block], g_in.at[pack], g_send.at[pack, block], g_recv.at[pack],
            earlier * 2 + block,
        )

    def boundary_part(pack, keep, send):
        for block in range(2):
            span = (2 - block) * tok
            scores, slopes = tile(pack, block, block, 2 - block)
            peak = stats[pack, block, 0:1]
            new_peak = jnp.maximum(peak, jnp.max(scores, axis=0, keepdims=True))
            factor = jnp.exp2(peak - new_peak)
            weights = jnp.exp2(scores - new_peak)
            total = stats[pack, block, 1:2] * factor + jnp.sum(weights, axis=0, keepdims=True)
            weighted = stats[pack, block, 2:3] * factor + jnp.sum(
                weights * slopes, axis=0, keepdims=True
            )
            inverse = 1.0 / total
            delta = weighted * inverse
            prob = weights * inverse
            prob_b = prob.astype(jnp.bfloat16)
            slope_b = (prob * (slopes - delta)).astype(jnp.bfloat16)
            if keep:
                norms[block, 0:1] = factor * inverse
                norms[block, 1:2] = delta
                p_low[block, :span] = prob_b
                s_low[block, :span] = slope_b
            if send:
                part_v = nn(prob_b, stacked(u_all, pack, block))
                part_k = nn(slope_b, stacked(q_all, pack, block))
                if block == 0:
                    carry_k, carry_v = part_k[tok:], part_v[tok:]
                    done_k, done_v = part_k[:tok], part_v[:tok]
                else:
                    done_k, done_v = carry_k + part_k, carry_v + part_v
                g_back[pack, block, 0] = done_k.astype(jnp.bfloat16)
                g_back[pack, block, 1] = done_v.astype(jnp.bfloat16)
                if block == 0:
                    pl.when(chip != 1)(back_copy(pack, 0).start)
                else:
                    back_copy(pack, 1).start()
                    pl.when(chip == 1)(back_copy(pack, 0).start)

    def no_boundary(pack):
        for block in range(2):
            inverse = 1.0 / stats[pack, block, 1:2]
            norms[block, 0:1] = inverse
            norms[block, 1:2] = stats[pack, block, 2:3] * inverse
            span = (2 - block) * tok
            p_low[block, :span] = jnp.zeros((span, heads * tok), jnp.bfloat16)
            s_low[block, :span] = jnp.zeros((span, heads * tok), jnp.bfloat16)

    def kv_in(pack):
        for block in range(2):
            remote(
                kv_own.at[0], kv_all.at[pack, block], kv_send.at[0], kv_recv.at[pack, block], mate
            ).wait_recv()

    passed = remote(kv_all.at[0, pl.ds(0, 2)], kv_all.at[0, pl.ds(0, 2)], pass_send, pass_recv, mate)

    for copy in loads[6:]:
        copy.wait()
    for copy in mates(0, peer):
        copy.wait_recv()

    @pl.when(has_later & (core == 1))
    def _():
        kv_out[1].start()


    @pl.when(core == 0)
    def _():
        local_part(0, True)

        @pl.when(has_earlier)
        def _():
            passed.wait_recv()
            boundary_part(0, True, False)

    @pl.when(core == 1)
    def _():
        local_part(0, False)
        for copy in mates(1, 0):
            copy.wait_recv()
        local_part(1, True)

        @pl.when(has_earlier)
        def _():
            kv_in(0)
            passed.start()
            boundary_part(0, False, True)
            kv_in(1)
            boundary_part(1, True, True)

    @pl.when(jnp.logical_not(has_earlier))
    def _():
        no_boundary(core)

    for block in range(2):
        span = (block + 1) * tok
        row = (2 - block) * tok
        prob = e_loc[block, :span] * norms[block, 0:1]
        prob_b = prob.astype(jnp.bfloat16)
        slope_b = (prob * (d_loc[block, :span] - norms[block, 1:2])).astype(jnp.bfloat16)
        p_low[block, row:] = prob_b
        s_low[block, row:] = slope_b
        part_v = nn(prob_b, stacked(u_all, core, block))
        part_k = nn(slope_b, stacked(q_all, core, block))
        if block == 0:
            carry_k, carry_v = part_k, part_v
        else:
            g_mine[0, 0] = carry_k + part_k[:tok]
            g_mine[0, 1] = carry_v + part_v[:tok]
            g_mine[1, 0] = part_k[tok:]
            g_mine[1, 1] = part_v[tok:]
    swap = remote(g_mine.at[peer], g_mate, gm_send, gm_recv, mate)
    swap.start()

    for block in range(2):
        keys = kv_all[core, block : block + 3, 0].reshape(3 * tok, HEAD)
        vals = kv_all[core, block : block + 3, 1].reshape(3 * tok, HEAD)
        out_t = nn(jnp.transpose(vals), p_low[block]).astype(jnp.bfloat16)
        gq_t = (nn(jnp.transpose(keys), s_low[block]) * scale).astype(jnp.bfloat16)
        for h in range(heads):
            cols = slice(h * HEAD, (h + 1) * HEAD)
            rows = slice(h * tok, (h + 1) * tok)
            out_buf[block, :, cols] = jnp.transpose(out_t[:, rows])
            gq_buf[block, :, cols] = jnp.transpose(gq_t[:, rows])
    outs = [
        remote(out_buf.at[peer], out_fin.at[core], o_send.at[0], o_recv.at[0], mate),
        remote(gq_buf.at[peer], gq_fin.at[core], o_send.at[1], o_recv.at[1], mate),
    ]
    stores = [
        pltpu.make_async_copy(out_buf.at[core], out_fin.at[core], store_sem.at[0]),
        pltpu.make_async_copy(gq_buf.at[core], gq_fin.at[core], store_sem.at[1]),
    ]
    for copy in outs + stores:
        copy.start()

    swap.wait_recv()
    for copy in (
        remote(out_buf.at[core], out_fin.at[peer], o_send.at[0], o_recv.at[0], mate),
        remote(gq_buf.at[core], gq_fin.at[peer], o_send.at[1], o_recv.at[1], mate),
    ):
        copy.wait_recv()
    for copy in stores:
        copy.wait()
    for copy in mate_out[0] + outs + [swap]:
        copy.wait_send()

    @pl.when(core == 0)
    def _():
        for copy in mate_out[1]:
            copy.wait_send()

    @pl.when(has_later)
    def _():
        for copy in kv_out:
            copy.wait_send()

    @pl.when(has_earlier & (core == 1))
    def _():
        passed.wait_send()
        for pack in range(2):
            for block in range(2):
                back_copy(pack, block).wait_send()

    mine = g_mine[pl.ds(core, 1)][0]
    for pack in range(2):
        own = core == pack
        sum_k = jnp.where(own, mine[0], g_mate[0])
        sum_v = jnp.where(own, mine[1], g_mate[1])
        pl.when(has_later)(
            remote(
                g_back.at[pack, 0], g_in.at[pack], g_send.at[pack, 0], g_recv.at[pack], mate
            ).wait_recv
        )
        gk_fin[pack] = ((sum_k + g_in[pack, 0].astype(jnp.float32)) * scale).astype(jnp.bfloat16)
        gv_fin[pack] = (sum_v + g_in[pack, 1].astype(jnp.float32)).astype(jnp.bfloat16)


def store(*refs):
    count = (len(refs) - 1) // 2
    copies = [
        pltpu.make_async_copy(refs[i], refs[count + i], refs[-1].at[i]) for i in range(count)
    ]
    for copy in copies:
        copy.start()
    for copy in copies:
        copy.wait()


def per_device(queries, keys, values, upstream, doc_ids):
    packs, tok, features = queries.shape
    heads = features // HEAD
    bf16, f32 = jnp.bfloat16, jnp.float32
    wide = heads * tok
    dma = pltpu.SemaphoreType.DMA
    anywhere = pl.BlockSpec(memory_space=pl.ANY)
    shapes = (queries.shape, queries.shape, keys.shape, keys.shape)
    results = pl.pallas_call(
        kernel,
        out_shape=tuple(pltpu.VMEM(shape, bf16) for shape in shapes),
        in_specs=[anywhere] * 5,
        out_specs=(pl.BlockSpec(memory_space=pltpu.VMEM),) * 4,
        scratch_shapes=[
            pltpu.VMEM((2, 2, tok, features), bf16),
            pltpu.VMEM((2, 2, tok, features), bf16),
            pltpu.VMEM((2, 4, 2, tok, HEAD), bf16),
            pltpu.VMEM((2, 2, tok, HEAD), bf16),
            pltpu.VMEM((2, 4 * tok), jnp.int32),
            pltpu.VMEM((2, 2, 3 * tok, tok), f32),
            pltpu.VMEM((2, 2, 8, wide), f32),
            pltpu.VMEM((2, 8, wide), f32),
            pltpu.VMEM((2, 2 * tok, wide), f32),
            pltpu.VMEM((2, 2 * tok, wide), f32),
            pltpu.VMEM((2, 3 * tok, wide), bf16),
            pltpu.VMEM((2, 3 * tok, wide), bf16),
            pltpu.VMEM((2, 2, 2, tok, HEAD), bf16),
            pltpu.VMEM((2, 2, tok, HEAD), bf16),
            pltpu.VMEM((2, 2, tok, HEAD), f32),
            pltpu.VMEM((2, tok, HEAD), f32),
            pltpu.VMEM((2, tok, features), bf16),
            pltpu.VMEM((2, tok, features), bf16),
            dma((10,)),
            dma((2,)),
            dma((2, 2)),
            dma((2, 3)),
            dma((2, 3)),
            dma(()),
            dma(()),
            dma((2, 2)),
            dma((2,)),
            dma(()),
            dma(()),
            dma((2,)),
            dma((2,)),
            dma((2,)),
        ],
        compiler_params=pltpu.CompilerParams(
            collective_id=0, has_side_effects=True, vmem_limit_bytes=60 * 1024 * 1024
        ),
        name="attention_both_ways",
    )(queries, keys, values, upstream, doc_ids)
    return pl.pallas_call(
        store,
        out_shape=tuple(jax.ShapeDtypeStruct(shape, bf16) for shape in shapes),
        in_specs=[anywhere] * 4,
        out_specs=(anywhere,) * 4,
        scratch_shapes=[dma((4,))],
        compiler_params=pltpu.CompilerParams(vmem_limit_bytes=4 * 1024 * 1024),
        name="store_results",
    )(*results)


def solution(mesh):
    return jax.shard_map(
        per_device,
        mesh=mesh,
        in_specs=(P("dp", "ctx", None),) * 4 + (P("dp", None),),
        out_specs=(P("dp", "ctx", None),) * 4,
        check_vma=False,
    )
```

```python
import math

import jax
import jax.numpy as jnp
from jax import lax
from jax.experimental import pallas as pl
from jax.experimental.pallas import tpu as pltpu
from jax.sharding import PartitionSpec as P

MESH = pl.DeviceIdType.MESH
NEG_LARGE = -1e30
HEAD = 128


def nt(a, b):
    return lax.dot_general(a, b, (((1,), (1,)), ((), ())), preferred_element_type=jnp.float32)


def nn(a, b):
    return lax.dot_general(a, b, (((1,), (0,)), ((), ())), preferred_element_type=jnp.float32)


def kernel(
    q_hbm, k_hbm, v_hbm, u_hbm, ids_hbm,
    out_fin, gq_fin, gk_fin, gv_fin,
    q_all, u_all, kv_all, kv_own, ids_v, bias, stats, norms,
    e_loc, d_loc, p_low, s_low,
    g_back, g_in, g_mine, g_mate, out_buf, gq_buf,
    load_sem, kv_send, kv_recv, mate_send, mate_recv, pass_send, pass_recv,
    g_send, g_recv, gm_send, gm_recv, o_send, o_recv, store_sem,
):
    tok = q_all.shape[2]
    heads = q_all.shape[3] // HEAD
    scale = HEAD**-0.5
    log2_scale = scale * math.log2(math.e)
    ctx = lax.axis_index("ctx")
    dp = lax.axis_index("dp")
    chips = lax.axis_size("ctx") // 2
    chip = ctx // 2
    core = ctx % 2
    peer = 1 - core
    mate = chip * 2 + peer
    has_later = chip < chips - 1
    has_earlier = chip > 0
    later = lax.rem(chip + 1, chips)
    earlier = lax.rem(chip + chips - 1, chips)

    def remote(src, dst, send, recv, target):
        return pltpu.make_async_remote_copy(
            src_ref=src, dst_ref=dst, send_sem=send, recv_sem=recv,
            device_id=(dp, target), device_id_type=MESH,
        )

    barrier = pltpu.get_barrier_semaphore()

    @pl.when(has_earlier & (core == 1))
    def _():
        for target in (earlier * 2 + 1, earlier * 2):
            pl.semaphore_signal(barrier, inc=1, device_id=(dp, target), device_id_type=MESH)

    pl.semaphore_signal(barrier, inc=1, device_id=(dp, mate), device_id_type=MESH)

    ids_first = pl.multiple_of(earlier * 2 * tok, 2 * tok)
    ids_own = pl.multiple_of(chip * 2 * tok, 2 * tok)
    pairs = [
        (k_hbm.at[0], kv_own.at[0, 0]),
        (v_hbm.at[0], kv_own.at[0, 1]),
        (k_hbm.at[1], kv_own.at[1, 0]),
        (v_hbm.at[1], kv_own.at[1, 1]),
        (ids_hbm.at[:, pl.ds(ids_first, 2 * tok)], ids_v.at[:, pl.ds(0, 2 * tok)]),
        (ids_hbm.at[:, pl.ds(ids_own, 2 * tok)], ids_v.at[:, pl.ds(2 * tok, 2 * tok)]),
        (q_hbm, q_all.at[:, core]),
        (u_hbm, u_all.at[:, core]),
        (k_hbm, kv_all.at[:, 2 + core, 0]),
        (v_hbm, kv_all.at[:, 2 + core, 1]),
    ]
    loads = [
        pltpu.make_async_copy(src, dst, load_sem.at[i]) for i, (src, dst) in enumerate(pairs)
    ]
    for copy in loads:
        copy.start()

    @pl.when(jnp.logical_not(has_earlier))
    def _():
        for pack in range(2):
            kv_all[pack, 0:2] = jnp.zeros((2,) + kv_all.shape[2:], kv_all.dtype)

    @pl.when(jnp.logical_not(has_later))
    def _():
        g_in[...] = jnp.zeros(g_in.shape, g_in.dtype)

    kv_out = [
        remote(
            kv_own.at[pack], kv_all.at[pack, core], kv_send.at[pack], kv_recv.at[pack, core],
            later * 2 + 1,
        )
        for pack in range(2)
    ]

    @pl.when(core == 0)
    def _():
        pl.semaphore_wait(barrier, jnp.where(has_later, 2, 1))

        @pl.when(has_later)
        def _():
            for i, src in enumerate((k_hbm, v_hbm)):
                remote(
                    src.at[0], kv_all.at[0, 0, i], kv_send.at[0], kv_recv.at[0, 0], later * 2 + 1
                ).start()


    @pl.when(core == 1)
    def _():
        for copy in loads[:4]:
            copy.wait()
        pl.semaphore_wait(barrier, jnp.where(has_later, 2, 1))
        pl.when(has_later)(kv_out[0].start)

    def mates(pack, block):
        return [
            remote(src.at[pack], dst, mate_send.at[pack, i], mate_recv.at[pack, i], mate)
            for i, (src, dst) in enumerate(
                (
                    (kv_own, kv_all.at[pack, 2 + block]),
                    (q_hbm, q_all.at[pack, block]),
                    (u_hbm, u_all.at[pack, block]),
                )
            )
        ]

    mate_out = [mates(0, core), mates(1, 0)]
    for copy in mate_out[0][1:]:
        copy.start()

    @pl.when(core == 0)
    def _():
        for copy in loads[:4]:
            copy.wait()

    mate_out[0][0].start()

    @pl.when(core == 0)
    def _():
        pl.when(has_later)(kv_out[1].start)
        for copy in mate_out[1]:
            copy.start()

    for copy in loads[4:6]:
        copy.wait()
    ids_two = ids_v[...]
    for pack in range(2):
        ids_row = ids_two[pack : pack + 1]
        lane = lax.broadcasted_iota(jnp.int32, ids_row.shape, 1)
        ids_row = jnp.where((lane < 2 * tok) & (chip == 0), -1, ids_row)
        ids_col = jnp.transpose(jnp.broadcast_to(ids_row, (tok, 4 * tok)))
        for block in range(2):
            first = block * tok
            q_first = (2 + block) * tok
            key_pos = first + lax.broadcasted_iota(jnp.int32, (3 * tok, tok), 0)
            query_pos = q_first + lax.broadcasted_iota(jnp.int32, (3 * tok, tok), 1)
            allowed = (ids_col[first : first + 3 * tok] == ids_row[:, q_first : q_first + tok]) & (
                key_pos <= query_pos
            )
            bias[pack, block] = jnp.where(allowed, 0.0, NEG_LARGE)

    def stacked(ref, pack, block):
        return jnp.concatenate(
            [ref[pack, block, :, h * HEAD : (h + 1) * HEAD] for h in range(heads)], axis=0
        )

    def tile(pack, block, key_first, key_blocks):
        span = key_blocks * tok
        keys = kv_all[pack, key_first : key_first + key_blocks, 0].reshape(span, HEAD)
        vals = kv_all[pack, key_first : key_first + key_blocks, 1].reshape(span, HEAD)
        row = (key_first - block) * tok
        add = bias[pack, block, row : row + span]
        scores = nt(keys, stacked(q_all, pack, block))
        slopes = nt(vals, stacked(u_all, pack, block))
        scores = scores * log2_scale + jnp.concatenate([add] * heads, axis=1)
        return scores, slopes

    def local_part(pack, keep):
        for block in range(2):
            span = (block + 1) * tok
            scores, slopes = tile(pack, block, 2, block + 1)
            peak = jnp.max(scores, axis=0, keepdims=True)
            weights = jnp.exp2(scores - peak)
            if keep:
                e_loc[block, :span] = weights
                d_loc[block, :span] = slopes
            stats[pack, block, 0:1] = peak
            stats[pack, block, 1:2] = jnp.sum(weights, axis=0, keepdims=True)
            stats[pack, block, 2:3] = jnp.sum(weights * slopes, axis=0, keepdims=True)

    def back_copy(pack, block):
        return remote(
            g_back.at[pack, block], g_in.at[pack], g_send.at[pack, block], g_recv.at[pack],
            earlier * 2 + block,
        )

    def boundary_part(pack, keep, send):
        for block in range(2):
            span = (2 - block) * tok
            scores, slopes = tile(pack, block, block, 2 - block)
            peak = stats[pack, block, 0:1]
            new_peak = jnp.maximum(peak, jnp.max(scores, axis=0, keepdims=True))
            factor = jnp.exp2(peak - new_peak)
            weights = jnp.exp2(scores - new_peak)
            total = stats[pack, block, 1:2] * factor + jnp.sum(weights, axis=0, keepdims=True)
            weighted = stats[pack, block, 2:3] * factor + jnp.sum(
                weights * slopes, axis=0, keepdims=True
            )
            inverse = 1.0 / total
            delta = weighted * inverse
            prob = weights * inverse
            prob_b = prob.astype(jnp.bfloat16)
            slope_b = (prob * (slopes - delta)).astype(jnp.bfloat16)
            if keep:
                norms[block, 0:1] = factor * inverse
                norms[block, 1:2] = delta
                p_low[block, :span] = prob_b
                s_low[block, :span] = slope_b
            if send:
                part_v = nn(prob_b, stacked(u_all, pack, block))
                part_k = nn(slope_b, stacked(q_all, pack, block))
                if block == 0:
                    carry_k, carry_v = part_k[tok:], part_v[tok:]
                    done_k, done_v = part_k[:tok], part_v[:tok]
                else:
                    done_k, done_v = carry_k + part_k, carry_v + part_v
                g_back[pack, block, 0] = done_k.astype(jnp.bfloat16)
                g_back[pack, block, 1] = done_v.astype(jnp.bfloat16)
                if block == 0:
                    pl.when(chip != 1)(back_copy(pack, 0).start)
                else:
                    back_copy(pack, 1).start()
                    pl.when(chip == 1)(back_copy(pack, 0).start)

    def no_boundary(pack):
        for block in range(2):
            inverse = 1.0 / stats[pack, block, 1:2]
            norms[block, 0:1] = inverse
            norms[block, 1:2] = stats[pack, block, 2:3] * inverse
            span = (2 - block) * tok
            p_low[block, :span] = jnp.zeros((span, heads * tok), jnp.bfloat16)
            s_low[block, :span] = jnp.zeros((span, heads * tok), jnp.bfloat16)

    def kv_in(pack):
        for block in range(2):
            remote(
                kv_own.at[0], kv_all.at[pack, block], kv_send.at[0], kv_recv.at[pack, block], mate
            ).wait_recv()

    passed = remote(kv_all.at[0, pl.ds(0, 2)], kv_all.at[0, pl.ds(0, 2)], pass_send, pass_recv, mate)

    for copy in loads[6:]:
        copy.wait()
    for copy in mates(0, peer):
        copy.wait_recv()

    @pl.when(has_later & (core == 1))
    def _():
        kv_out[1].start()


    @pl.when(core == 0)
    def _():
        local_part(0, True)

        @pl.when(has_earlier)
        def _():
            passed.wait_recv()
            boundary_part(0, True, False)

    @pl.when(core == 1)
    def _():
        local_part(0, False)
        for copy in mates(1, 0):
            copy.wait_recv()
        local_part(1, True)

        @pl.when(has_earlier)
        def _():
            kv_in(0)
            passed.start()
            boundary_part(0, False, True)
            kv_in(1)
            boundary_part(1, True, True)

    @pl.when(jnp.logical_not(has_earlier))
    def _():
        no_boundary(core)

    for block in range(2):
        span = (block + 1) * tok
        row = (2 - block) * tok
        prob = e_loc[block, :span] * norms[block, 0:1]
        prob_b = prob.astype(jnp.bfloat16)
        slope_b = (prob * (d_loc[block, :span] - norms[block, 1:2])).astype(jnp.bfloat16)
        p_low[block, row:] = prob_b
        s_low[block, row:] = slope_b
        part_v = nn(prob_b, stacked(u_all, core, block))
        part_k = nn(slope_b, stacked(q_all, core, block))
        if block == 0:
            carry_k, carry_v = part_k, part_v
        else:
            g_mine[0, 0] = carry_k + part_k[:tok]
            g_mine[0, 1] = carry_v + part_v[:tok]
            g_mine[1, 0] = part_k[tok:]
            g_mine[1, 1] = part_v[tok:]
    swap = remote(g_mine.at[peer], g_mate, gm_send, gm_recv, mate)
    swap.start()

    for block in range(2):
        keys = kv_all[core, block : block + 3, 0].reshape(3 * tok, HEAD)
        vals = kv_all[core, block : block + 3, 1].reshape(3 * tok, HEAD)
        out_t = nn(jnp.transpose(vals), p_low[block]).astype(jnp.bfloat16)
        gq_t = (nn(jnp.transpose(keys), s_low[block]) * scale).astype(jnp.bfloat16)
        for h in range(heads):
            cols = slice(h * HEAD, (h + 1) * HEAD)
            rows = slice(h * tok, (h + 1) * tok)
            out_buf[block, :, cols] = jnp.transpose(out_t[:, rows])
            gq_buf[block, :, cols] = jnp.transpose(gq_t[:, rows])
    outs = [
        remote(out_buf.at[peer], out_fin.at[core], o_send.at[0], o_recv.at[0], mate),
        remote(gq_buf.at[peer], gq_fin.at[core], o_send.at[1], o_recv.at[1], mate),
    ]
    stores = [
        pltpu.make_async_copy(out_buf.at[core], out_fin.at[core], store_sem.at[0]),
        pltpu.make_async_copy(gq_buf.at[core], gq_fin.at[core], store_sem.at[1]),
    ]
    for copy in outs + stores:
        copy.start()

    swap.wait_recv()
    for copy in (
        remote(out_buf.at[core], out_fin.at[peer], o_send.at[0], o_recv.at[0], mate),
        remote(gq_buf.at[core], gq_fin.at[peer], o_send.at[1], o_recv.at[1], mate),
    ):
        copy.wait_recv()
    for copy in stores:
        copy.wait()
    for copy in mate_out[0] + outs + [swap]:
        copy.wait_send()

    @pl.when(core == 0)
    def _():
        for copy in mate_out[1]:
            copy.wait_send()

    @pl.when(has_later)
    def _():
        for copy in kv_out:
            copy.wait_send()

    @pl.when(has_earlier & (core == 1))
    def _():
        passed.wait_send()
        for pack in range(2):
            for block in range(2):
                back_copy(pack, block).wait_send()

    mine = g_mine[pl.ds(core, 1)][0]
    for pack in range(2):
        own = core == pack
        sum_k = jnp.where(own, mine[0], g_mate[0])
        sum_v = jnp.where(own, mine[1], g_mate[1])
        pl.when(has_later)(
            remote(
                g_back.at[pack, 0], g_in.at[pack], g_send.at[pack, 0], g_recv.at[pack], mate
            ).wait_recv
        )
        gk_fin[pack] = ((sum_k + g_in[pack, 0].astype(jnp.float32)) * scale).astype(jnp.bfloat16)
        gv_fin[pack] = (sum_v + g_in[pack, 1].astype(jnp.float32)).astype(jnp.bfloat16)


def store(*refs):
    count = (len(refs) - 1) // 2
    copies = [
        pltpu.make_async_copy(refs[i], refs[count + i], refs[-1].at[i]) for i in range(count)
    ]
    for copy in copies:
        copy.start()
    for copy in copies:
        copy.wait()


def per_device(queries, keys, values, upstream, doc_ids):
    packs, tok, features = queries.shape
    heads = features // HEAD
    bf16, f32 = jnp.bfloat16, jnp.float32
    wide = heads * tok
    dma = pltpu.SemaphoreType.DMA
    anywhere = pl.BlockSpec(memory_space=pl.ANY)
    shapes = (queries.shape, queries.shape, keys.shape, keys.shape)
    results = pl.pallas_call(
        kernel,
        out_shape=tuple(pltpu.VMEM(shape, bf16) for shape in shapes),
        in_specs=[anywhere] * 5,
        out_specs=(pl.BlockSpec(memory_space=pltpu.VMEM),) * 4,
        scratch_shapes=[
            pltpu.VMEM((2, 2, tok, features), bf16),
            pltpu.VMEM((2, 2, tok, features), bf16),
            pltpu.VMEM((2, 4, 2, tok, HEAD), bf16),
            pltpu.VMEM((2, 2, tok, HEAD), bf16),
            pltpu.VMEM((2, 4 * tok), jnp.int32),
            pltpu.VMEM((2, 2, 3 * tok, tok), f32),
            pltpu.VMEM((2, 2, 8, wide), f32),
            pltpu.VMEM((2, 8, wide), f32),
            pltpu.VMEM((2, 2 * tok, wide), f32),
            pltpu.VMEM((2, 2 * tok, wide), f32),
            pltpu.VMEM((2, 3 * tok, wide), bf16),
            pltpu.VMEM((2, 3 * tok, wide), bf16),
            pltpu.VMEM((2, 2, 2, tok, HEAD), bf16),
            pltpu.VMEM((2, 2, tok, HEAD), bf16),
            pltpu.VMEM((2, 2, tok, HEAD), f32),
            pltpu.VMEM((2, tok, HEAD), f32),
            pltpu.VMEM((2, tok, features), bf16),
            pltpu.VMEM((2, tok, features), bf16),
            dma((10,)),
            dma((2,)),
            dma((2, 2)),
            dma((2, 3)),
            dma((2, 3)),
            dma(()),
            dma(()),
            dma((2, 2)),
            dma((2,)),
            dma(()),
            dma(()),
            dma((2,)),
            dma((2,)),
            dma((2,)),
        ],
        compiler_params=pltpu.CompilerParams(
            collective_id=0, has_side_effects=True, vmem_limit_bytes=60 * 1024 * 1024
        ),
        name="attention_both_ways",
    )(queries, keys, values, upstream, doc_ids)
    return pl.pallas_call(
        store,
        out_shape=tuple(jax.ShapeDtypeStruct(shape, bf16) for shape in shapes),
        in_specs=[anywhere] * 4,
        out_specs=(anywhere,) * 4,
        scratch_shapes=[dma((4,))],
        compiler_params=pltpu.CompilerParams(vmem_limit_bytes=4 * 1024 * 1024),
        name="store_results",
    )(*results)


def solution(mesh):
    return jax.shard_map(
        per_device,
        mesh=mesh,
        in_specs=(P("dp", "ctx", None),) * 4 + (P("dp", None),),
        out_specs=(P("dp", "ctx", None),) * 4,
        check_vma=False,
    )
```

```python
import math

import jax
import jax.numpy as jnp
from jax import lax
from jax.experimental import pallas as pl
from jax.experimental.pallas import tpu as pltpu
from jax.sharding import PartitionSpec as P

MESH = pl.DeviceIdType.MESH
NEG_LARGE = -1e30
HEAD = 128


def nt(a, b):
    return lax.dot_general(a, b, (((1,), (1,)), ((), ())), preferred_element_type=jnp.float32)


def nn(a, b):
    return lax.dot_general(a, b, (((1,), (0,)), ((), ())), preferred_element_type=jnp.float32)


def kernel(
    q_hbm, k_hbm, v_hbm, u_hbm, ids_hbm,
    out_fin, gq_fin, gk_fin, gv_fin,
    q_all, u_all, kv_all, kv_own, ids_v, bias, stats, norms,
    e_loc, d_loc, p_low, s_low,
    g_back, g_in, g_mine, g_mate, out_buf, gq_buf,
    load_sem, kv_send, kv_recv, mate_send, mate_recv, pass_send, pass_recv,
    g_send, g_recv, gm_send, gm_recv, o_send, o_recv, store_sem,
):
    tok = q_all.shape[2]
    heads = q_all.shape[3] // HEAD
    scale = HEAD**-0.5
    log2_scale = scale * math.log2(math.e)
    ctx = lax.axis_index("ctx")
    dp = lax.axis_index("dp")
    chips = lax.axis_size("ctx") // 2
    chip = ctx // 2
    core = ctx % 2
    peer = 1 - core
    mate = chip * 2 + peer
    has_later = chip < chips - 1
    has_earlier = chip > 0
    later = lax.rem(chip + 1, chips)
    earlier = lax.rem(chip + chips - 1, chips)

    def remote(src, dst, send, recv, target):
        return pltpu.make_async_remote_copy(
            src_ref=src, dst_ref=dst, send_sem=send, recv_sem=recv,
            device_id=(dp, target), device_id_type=MESH,
        )

    barrier = pltpu.get_barrier_semaphore()

    @pl.when(has_earlier & (core == 1))
    def _():
        for target in (earlier * 2 + 1, earlier * 2):
            pl.semaphore_signal(barrier, inc=1, device_id=(dp, target), device_id_type=MESH)

    pl.semaphore_signal(barrier, inc=1, device_id=(dp, mate), device_id_type=MESH)

    ids_first = pl.multiple_of(earlier * 2 * tok, 2 * tok)
    ids_own = pl.multiple_of(chip * 2 * tok, 2 * tok)
    pairs = [
        (k_hbm.at[0], kv_own.at[0, 0]),
        (v_hbm.at[0], kv_own.at[0, 1]),
        (k_hbm.at[1], kv_own.at[1, 0]),
        (v_hbm.at[1], kv_own.at[1, 1]),
        (ids_hbm.at[:, pl.ds(ids_first, 2 * tok)], ids_v.at[:, pl.ds(0, 2 * tok)]),
        (ids_hbm.at[:, pl.ds(ids_own, 2 * tok)], ids_v.at[:, pl.ds(2 * tok, 2 * tok)]),
        (q_hbm, q_all.at[:, core]),
        (u_hbm, u_all.at[:, core]),
        (k_hbm, kv_all.at[:, 2 + core, 0]),
        (v_hbm, kv_all.at[:, 2 + core, 1]),
    ]
    loads = [
        pltpu.make_async_copy(src, dst, load_sem.at[i]) for i, (src, dst) in enumerate(pairs)
    ]
    for copy in loads[:4]:
        copy.start()

    @pl.when(core == 1)
    def _():
        for copy in loads[4:]:
            copy.start()

    @pl.when(jnp.logical_not(has_earlier))
    def _():
        for pack in range(2):
            kv_all[pack, 0:2] = jnp.zeros((2,) + kv_all.shape[2:], kv_all.dtype)

    @pl.when(jnp.logical_not(has_later))
    def _():
        g_in[...] = jnp.zeros(g_in.shape, g_in.dtype)

    kv_out = [
        remote(
            kv_own.at[pack], kv_all.at[pack, core], kv_send.at[pack], kv_recv.at[pack, core],
            later * 2 + 1,
        )
        for pack in range(2)
    ]

    @pl.when(core == 0)
    def _():
        pl.semaphore_wait(barrier, jnp.where(has_later, 2, 1))

        @pl.when(has_later)
        def _():
            for i, src in enumerate((k_hbm, v_hbm)):
                remote(
                    src.at[0], kv_all.at[0, 0, i], kv_send.at[0], kv_recv.at[0, 0], later * 2 + 1
                ).start()

        for copy in loads[4:]:
            copy.start()

    @pl.when(core == 1)
    def _():
        for copy in loads[:4]:
            copy.wait()
        pl.semaphore_wait(barrier, jnp.where(has_later, 2, 1))
        pl.when(has_later)(kv_out[0].start)

    def mates(pack, block):
        return [
            remote(src.at[pack], dst, mate_send.at[pack, i], mate_recv.at[pack, i], mate)
            for i, (src, dst) in enumerate(
                (
                    (kv_own, kv_all.at[pack, 2 + block]),
                    (q_hbm, q_all.at[pack, block]),
                    (u_hbm, u_all.at[pack, block]),
                )
            )
        ]

    mate_out = [mates(0, core), mates(1, 0)]
    for copy in mate_out[0][1:]:
        copy.start()

    @pl.when(core == 0)
    def _():
        for copy in loads[:4]:
            copy.wait()

    mate_out[0][0].start()

    @pl.when(core == 0)
    def _():
        pl.when(has_later)(kv_out[1].start)
        for copy in mate_out[1]:
            copy.start()

    for copy in loads[4:6]:
        copy.wait()
    ids_two = ids_v[...]
    for pack in range(2):
        ids_row = ids_two[pack : pack + 1]
        lane = lax.broadcasted_iota(jnp.int32, ids_row.shape, 1)
        ids_row = jnp.where((lane < 2 * tok) & (chip == 0), -1, ids_row)
        ids_col = jnp.transpose(jnp.broadcast_to(ids_row, (tok, 4 * tok)))
        for block in range(2):
            first = block * tok
            q_first = (2 + block) * tok
            key_pos = first + lax.broadcasted_iota(jnp.int32, (3 * tok, tok), 0)
            query_pos = q_first + lax.broadcasted_iota(jnp.int32, (3 * tok, tok), 1)
            allowed = (ids_col[first : first + 3 * tok] == ids_row[:, q_first : q_first + tok]) & (
                key_pos <= query_pos
            )
            bias[pack, block] = jnp.where(allowed, 0.0, NEG_LARGE)

    def stacked(ref, pack, block):
        return jnp.concatenate(
            [ref[pack, block, :, h * HEAD : (h + 1) * HEAD] for h in range(heads)], axis=0
        )

    def tile(pack, block, key_first, key_blocks):
        span = key_blocks * tok
        keys = kv_all[pack, key_first : key_first + key_blocks, 0].reshape(span, HEAD)
        vals = kv_all[pack, key_first : key_first + key_blocks, 1].reshape(span, HEAD)
        row = (key_first - block) * tok
        add = bias[pack, block, row : row + span]
        scores = nt(keys, stacked(q_all, pack, block))
        slopes = nt(vals, stacked(u_all, pack, block))
        scores = scores * log2_scale + jnp.concatenate([add] * heads, axis=1)
        return scores, slopes

    def local_part(pack, keep):
        for block in range(2):
            span = (block + 1) * tok
            scores, slopes = tile(pack, block, 2, block + 1)
            peak = jnp.max(scores, axis=0, keepdims=True)
            weights = jnp.exp2(scores - peak)
            if keep:
                e_loc[block, :span] = weights
                d_loc[block, :span] = slopes
            stats[pack, block, 0:1] = peak
            stats[pack, block, 1:2] = jnp.sum(weights, axis=0, keepdims=True)
            stats[pack, block, 2:3] = jnp.sum(weights * slopes, axis=0, keepdims=True)

    def back_copy(pack, block):
        return remote(
            g_back.at[pack, block], g_in.at[pack], g_send.at[pack, block], g_recv.at[pack],
            earlier * 2 + block,
        )

    def boundary_part(pack, keep, send):
        for block in range(2):
            span = (2 - block) * tok
            scores, slopes = tile(pack, block, block, 2 - block)
            peak = stats[pack, block, 0:1]
            new_peak = jnp.maximum(peak, jnp.max(scores, axis=0, keepdims=True))
            factor = jnp.exp2(peak - new_peak)
            weights = jnp.exp2(scores - new_peak)
            total = stats[pack, block, 1:2] * factor + jnp.sum(weights, axis=0, keepdims=True)
            weighted = stats[pack, block, 2:3] * factor + jnp.sum(
                weights * slopes, axis=0, keepdims=True
            )
            inverse = 1.0 / total
            delta = weighted * inverse
            prob = weights * inverse
            prob_b = prob.astype(jnp.bfloat16)
            slope_b = (prob * (slopes - delta)).astype(jnp.bfloat16)
            if keep:
                norms[block, 0:1] = factor * inverse
                norms[block, 1:2] = delta
                p_low[block, :span] = prob_b
                s_low[block, :span] = slope_b
            if send:
                part_v = nn(prob_b, stacked(u_all, pack, block))
                part_k = nn(slope_b, stacked(q_all, pack, block))
                if block == 0:
                    carry_k, carry_v = part_k[tok:], part_v[tok:]
                    done_k, done_v = part_k[:tok], part_v[:tok]
                else:
                    done_k, done_v = carry_k + part_k, carry_v + part_v
                g_back[pack, block, 0] = done_k.astype(jnp.bfloat16)
                g_back[pack, block, 1] = done_v.astype(jnp.bfloat16)
                if block == 0:
                    pl.when(chip != 1)(back_copy(pack, 0).start)
                else:
                    back_copy(pack, 1).start()
                    pl.when(chip == 1)(back_copy(pack, 0).start)

    def no_boundary(pack):
        for block in range(2):
            inverse = 1.0 / stats[pack, block, 1:2]
            norms[block, 0:1] = inverse
            norms[block, 1:2] = stats[pack, block, 2:3] * inverse
            span = (2 - block) * tok
            p_low[block, :span] = jnp.zeros((span, heads * tok), jnp.bfloat16)
            s_low[block, :span] = jnp.zeros((span, heads * tok), jnp.bfloat16)

    def kv_in(pack):
        for block in range(2):
            remote(
                kv_own.at[0], kv_all.at[pack, block], kv_send.at[0], kv_recv.at[pack, block], mate
            ).wait_recv()

    passed = remote(kv_all.at[0, pl.ds(0, 2)], kv_all.at[0, pl.ds(0, 2)], pass_send, pass_recv, mate)

    for copy in loads[6:]:
        copy.wait()
    for copy in mates(0, peer):
        copy.wait_recv()

    @pl.when(has_later & (core == 1))
    def _():
        kv_out[1].start()


    @pl.when(core == 0)
    def _():
        local_part(0, True)

        @pl.when(has_earlier)
        def _():
            passed.wait_recv()
            boundary_part(0, True, False)

    @pl.when(core == 1)
    def _():
        local_part(0, False)
        for copy in mates(1, 0):
            copy.wait_recv()
        local_part(1, True)

        @pl.when(has_earlier)
        def _():
            kv_in(0)
            passed.start()
            boundary_part(0, False, True)
            kv_in(1)
            boundary_part(1, True, True)

    @pl.when(jnp.logical_not(has_earlier))
    def _():
        no_boundary(core)

    for block in range(2):
        span = (block + 1) * tok
        row = (2 - block) * tok
        prob = e_loc[block, :span] * norms[block, 0:1]
        prob_b = prob.astype(jnp.bfloat16)
        slope_b = (prob * (d_loc[block, :span] - norms[block, 1:2])).astype(jnp.bfloat16)
        p_low[block, row:] = prob_b
        s_low[block, row:] = slope_b
        part_v = nn(prob_b, stacked(u_all, core, block))
        part_k = nn(slope_b, stacked(q_all, core, block))
        if block == 0:
            carry_k, carry_v = part_k, part_v
        else:
            g_mine[0, 0] = carry_k + part_k[:tok]
            g_mine[0, 1] = carry_v + part_v[:tok]
            g_mine[1, 0] = part_k[tok:]
            g_mine[1, 1] = part_v[tok:]
    swap = remote(g_mine.at[peer], g_mate, gm_send, gm_recv, mate)
    swap.start()

    for block in range(2):
        keys = kv_all[core, block : block + 3, 0].reshape(3 * tok, HEAD)
        vals = kv_all[core, block : block + 3, 1].reshape(3 * tok, HEAD)
        out_t = nn(jnp.transpose(vals), p_low[block]).astype(jnp.bfloat16)
        gq_t = (nn(jnp.transpose(keys), s_low[block]) * scale).astype(jnp.bfloat16)
        for h in range(heads):
            cols = slice(h * HEAD, (h + 1) * HEAD)
            rows = slice(h * tok, (h + 1) * tok)
            out_buf[block, :, cols] = jnp.transpose(out_t[:, rows])
            gq_buf[block, :, cols] = jnp.transpose(gq_t[:, rows])
    outs = [
        remote(out_buf.at[peer], out_fin.at[core], o_send.at[0], o_recv.at[0], mate),
        remote(gq_buf.at[peer], gq_fin.at[core], o_send.at[1], o_recv.at[1], mate),
    ]
    stores = [
        pltpu.make_async_copy(out_buf.at[core], out_fin.at[core], store_sem.at[0]),
        pltpu.make_async_copy(gq_buf.at[core], gq_fin.at[core], store_sem.at[1]),
    ]
    for copy in outs + stores:
        copy.start()

    swap.wait_recv()
    for copy in (
        remote(out_buf.at[core], out_fin.at[peer], o_send.at[0], o_recv.at[0], mate),
        remote(gq_buf.at[core], gq_fin.at[peer], o_send.at[1], o_recv.at[1], mate),
    ):
        copy.wait_recv()
    for copy in stores:
        copy.wait()
    for copy in mate_out[0] + outs + [swap]:
        copy.wait_send()

    @pl.when(core == 0)
    def _():
        for copy in mate_out[1]:
            copy.wait_send()

    @pl.when(has_later)
    def _():
        for copy in kv_out:
            copy.wait_send()

    @pl.when(has_earlier & (core == 1))
    def _():
        passed.wait_send()
        for pack in range(2):
            for block in range(2):
                back_copy(pack, block).wait_send()

    mine = g_mine[pl.ds(core, 1)][0]
    for pack in range(2):
        own = core == pack
        sum_k = jnp.where(own, mine[0], g_mate[0])
        sum_v = jnp.where(own, mine[1], g_mate[1])
        pl.when(has_later)(
            remote(
                g_back.at[pack, 0], g_in.at[pack], g_send.at[pack, 0], g_recv.at[pack], mate
            ).wait_recv
        )
        gk_fin[pack] = ((sum_k + g_in[pack, 0].astype(jnp.float32)) * scale).astype(jnp.bfloat16)
        gv_fin[pack] = (sum_v + g_in[pack, 1].astype(jnp.float32)).astype(jnp.bfloat16)


def store(*refs):
    count = (len(refs) - 1) // 2
    copies = [
        pltpu.make_async_copy(refs[i], refs[count + i], refs[-1].at[i]) for i in range(count)
    ]
    for copy in copies:
        copy.start()
    for copy in copies:
        copy.wait()


def per_device(queries, keys, values, upstream, doc_ids):
    packs, tok, features = queries.shape
    heads = features // HEAD
    bf16, f32 = jnp.bfloat16, jnp.float32
    wide = heads * tok
    dma = pltpu.SemaphoreType.DMA
    anywhere = pl.BlockSpec(memory_space=pl.ANY)
    shapes = (queries.shape, queries.shape, keys.shape, keys.shape)
    results = pl.pallas_call(
        kernel,
        out_shape=tuple(pltpu.VMEM(shape, bf16) for shape in shapes),
        in_specs=[anywhere] * 5,
        out_specs=(pl.BlockSpec(memory_space=pltpu.VMEM),) * 4,
        scratch_shapes=[
            pltpu.VMEM((2, 2, tok, features), bf16),
            pltpu.VMEM((2, 2, tok, features), bf16),
            pltpu.VMEM((2, 4, 2, tok, HEAD), bf16),
            pltpu.VMEM((2, 2, tok, HEAD), bf16),
            pltpu.VMEM((2, 4 * tok), jnp.int32),
            pltpu.VMEM((2, 2, 3 * tok, tok), f32),
            pltpu.VMEM((2, 2, 8, wide), f32),
            pltpu.VMEM((2, 8, wide), f32),
            pltpu.VMEM((2, 2 * tok, wide), f32),
            pltpu.VMEM((2, 2 * tok, wide), f32),
            pltpu.VMEM((2, 3 * tok, wide), bf16),
            pltpu.VMEM((2, 3 * tok, wide), bf16),
            pltpu.VMEM((2, 2, 2, tok, HEAD), bf16),
            pltpu.VMEM((2, 2, tok, HEAD), bf16),
            pltpu.VMEM((2, 2, tok, HEAD), f32),
            pltpu.VMEM((2, tok, HEAD), f32),
            pltpu.VMEM((2, tok, features), bf16),
            pltpu.VMEM((2, tok, features), bf16),
            dma((10,)),
            dma((2,)),
            dma((2, 2)),
            dma((2, 3)),
            dma((2, 3)),
            dma(()),
            dma(()),
            dma((2, 2)),
            dma((2,)),
            dma(()),
            dma(()),
            dma((2,)),
            dma((2,)),
            dma((2,)),
        ],
        compiler_params=pltpu.CompilerParams(
            collective_id=0, has_side_effects=True, vmem_limit_bytes=60 * 1024 * 1024
        ),
        name="attention_both_ways",
    )(queries, keys, values, upstream, doc_ids)
    return pl.pallas_call(
        store,
        out_shape=tuple(jax.ShapeDtypeStruct(shape, bf16) for shape in shapes),
        in_specs=[anywhere] * 4,
        out_specs=(anywhere,) * 4,
        scratch_shapes=[dma((4,))],
        compiler_params=pltpu.CompilerParams(vmem_limit_bytes=4 * 1024 * 1024),
        name="store_results",
    )(*results)


def solution(mesh):
    return jax.shard_map(
        per_device,
        mesh=mesh,
        in_specs=(P("dp", "ctx", None),) * 4 + (P("dp", None),),
        out_specs=(P("dp", "ctx", None),) * 4,
        check_vma=False,
    )
```

```python
import math

import jax
import jax.numpy as jnp
from jax import lax
from jax.experimental import pallas as pl
from jax.experimental.pallas import tpu as pltpu
from jax.sharding import PartitionSpec as P

MESH = pl.DeviceIdType.MESH
NEG_LARGE = -1e30
HEAD = 128


def nt(a, b):
    return lax.dot_general(a, b, (((1,), (1,)), ((), ())), preferred_element_type=jnp.float32)


def nn(a, b):
    return lax.dot_general(a, b, (((1,), (0,)), ((), ())), preferred_element_type=jnp.float32)


def kernel(
    q_hbm, k_hbm, v_hbm, u_hbm, ids_hbm,
    out_fin, gq_fin, gk_fin, gv_fin,
    q_all, u_all, kv_all, kv_own, ids_v, bias, stats, norms,
    e_loc, d_loc, p_low, s_low,
    g_back, g_in, g_mine, g_mate, out_buf, gq_buf,
    load_sem, kv_send, kv_recv, mate_send, mate_recv, pass_send, pass_recv,
    g_send, g_recv, gm_send, gm_recv, o_send, o_recv, store_sem,
):
    tok = q_all.shape[2]
    heads = q_all.shape[3] // HEAD
    scale = HEAD**-0.5
    log2_scale = scale * math.log2(math.e)
    ctx = lax.axis_index("ctx")
    dp = lax.axis_index("dp")
    chips = lax.axis_size("ctx") // 2
    chip = ctx // 2
    core = ctx % 2
    peer = 1 - core
    mate = chip * 2 + peer
    has_later = chip < chips - 1
    has_earlier = chip > 0
    later = lax.rem(chip + 1, chips)
    earlier = lax.rem(chip + chips - 1, chips)

    def remote(src, dst, send, recv, target):
        return pltpu.make_async_remote_copy(
            src_ref=src, dst_ref=dst, send_sem=send, recv_sem=recv,
            device_id=(dp, target), device_id_type=MESH,
        )

    barrier = pltpu.get_barrier_semaphore()

    @pl.when(has_earlier & (core == 1))
    def _():
        for target in (earlier * 2 + 1, earlier * 2):
            pl.semaphore_signal(barrier, inc=1, device_id=(dp, target), device_id_type=MESH)

    pl.semaphore_signal(barrier, inc=1, device_id=(dp, mate), device_id_type=MESH)

    ids_first = pl.multiple_of(earlier * 2 * tok, 2 * tok)
    ids_own = pl.multiple_of(chip * 2 * tok, 2 * tok)
    pairs = [
        (k_hbm.at[0], kv_own.at[0, 0]),
        (v_hbm.at[0], kv_own.at[0, 1]),
        (k_hbm.at[1], kv_own.at[1, 0]),
        (v_hbm.at[1], kv_own.at[1, 1]),
        (ids_hbm.at[:, pl.ds(ids_first, 2 * tok)], ids_v.at[:, pl.ds(0, 2 * tok)]),
        (ids_hbm.at[:, pl.ds(ids_own, 2 * tok)], ids_v.at[:, pl.ds(2 * tok, 2 * tok)]),
        (q_hbm, q_all.at[:, core]),
        (u_hbm, u_all.at[:, core]),
        (k_hbm, kv_all.at[:, 2 + core, 0]),
        (v_hbm, kv_all.at[:, 2 + core, 1]),
    ]
    loads = [
        pltpu.make_async_copy(src, dst, load_sem.at[i]) for i, (src, dst) in enumerate(pairs)
    ]
    for copy in loads:
        copy.start()

    @pl.when(jnp.logical_not(has_earlier))
    def _():
        for pack in range(2):
            kv_all[pack, 0:2] = jnp.zeros((2,) + kv_all.shape[2:], kv_all.dtype)

    @pl.when(jnp.logical_not(has_later))
    def _():
        g_in[...] = jnp.zeros(g_in.shape, g_in.dtype)

    kv_out = [
        remote(
            kv_own.at[pack], kv_all.at[pack, core], kv_send.at[pack], kv_recv.at[pack, core],
            later * 2 + 1,
        )
        for pack in range(2)
    ]

    @pl.when(core == 0)
    def _():
        pl.semaphore_wait(barrier, jnp.where(has_later, 2, 1))

        @pl.when(has_later)
        def _():
            for i, src in enumerate((k_hbm, v_hbm)):
                remote(
                    src.at[0], kv_all.at[0, 0, i], kv_send.at[0], kv_recv.at[0, 0], later * 2 + 1
                ).start()


    @pl.when(core == 1)
    def _():
        for copy in loads[:4]:
            copy.wait()
        pl.semaphore_wait(barrier, jnp.where(has_later, 2, 1))
        pl.when(has_later)(kv_out[0].start)

    def mates(pack, block):
        return [
            remote(src.at[pack], dst, mate_send.at[pack, i], mate_recv.at[pack, i], mate)
            for i, (src, dst) in enumerate(
                (
                    (kv_own, kv_all.at[pack, 2 + block]),
                    (q_hbm, q_all.at[pack, block]),
                    (u_hbm, u_all.at[pack, block]),
                )
            )
        ]

    mate_out = [mates(0, core), mates(1, 0)]
    for copy in mate_out[0][1:]:
        copy.start()

    @pl.when(core == 0)
    def _():
        for copy in loads[:4]:
            copy.wait()

    mate_out[0][0].start()

    @pl.when(core == 0)
    def _():
        pl.when(has_later)(kv_out[1].start)
        for copy in mate_out[1]:
            copy.start()

    for copy in loads[4:6]:
        copy.wait()
    ids_two = ids_v[...]
    for pack in range(2):
        ids_row = ids_two[pack : pack + 1]
        lane = lax.broadcasted_iota(jnp.int32, ids_row.shape, 1)
        ids_row = jnp.where((lane < 2 * tok) & (chip == 0), -1, ids_row)
        ids_col = jnp.transpose(jnp.broadcast_to(ids_row, (tok, 4 * tok)))
        for block in range(2):
            first = block * tok
            q_first = (2 + block) * tok
            key_pos = first + lax.broadcasted_iota(jnp.int32, (3 * tok, tok), 0)
            query_pos = q_first + lax.broadcasted_iota(jnp.int32, (3 * tok, tok), 1)
            allowed = (ids_col[first : first + 3 * tok] == ids_row[:, q_first : q_first + tok]) & (
                key_pos <= query_pos
            )
            bias[pack, block] = jnp.where(allowed, 0.0, NEG_LARGE)

    def stacked(ref, pack, block):
        return jnp.concatenate(
            [ref[pack, block, :, h * HEAD : (h + 1) * HEAD] for h in range(heads)], axis=0
        )

    def tile(pack, block, key_first, key_blocks):
        span = key_blocks * tok
        keys = kv_all[pack, key_first : key_first + key_blocks, 0].reshape(span, HEAD)
        vals = kv_all[pack, key_first : key_first + key_blocks, 1].reshape(span, HEAD)
        row = (key_first - block) * tok
        add = bias[pack, block, row : row + span]
        scores = nt(keys, stacked(q_all, pack, block))
        slopes = nt(vals, stacked(u_all, pack, block))
        scores = scores * log2_scale + jnp.concatenate([add] * heads, axis=1)
        return scores, slopes

    def local_part(pack, keep):
        for block in range(2):
            span = (block + 1) * tok
            scores, slopes = tile(pack, block, 2, block + 1)
            peak = jnp.max(scores, axis=0, keepdims=True)
            weights = jnp.exp2(scores - peak)
            if keep:
                e_loc[block, :span] = weights
                d_loc[block, :span] = slopes
            stats[pack, block, 0:1] = peak
            stats[pack, block, 1:2] = jnp.sum(weights, axis=0, keepdims=True)
            stats[pack, block, 2:3] = jnp.sum(weights * slopes, axis=0, keepdims=True)

    def back_copy(pack, block):
        return remote(
            g_back.at[pack, block], g_in.at[pack], g_send.at[pack, block], g_recv.at[pack],
            earlier * 2 + block,
        )

    def boundary_part(pack, keep, send):
        for block in range(2):
            span = (2 - block) * tok
            scores, slopes = tile(pack, block, block, 2 - block)
            peak = stats[pack, block, 0:1]
            new_peak = jnp.maximum(peak, jnp.max(scores, axis=0, keepdims=True))
            factor = jnp.exp2(peak - new_peak)
            weights = jnp.exp2(scores - new_peak)
            total = stats[pack, block, 1:2] * factor + jnp.sum(weights, axis=0, keepdims=True)
            weighted = stats[pack, block, 2:3] * factor + jnp.sum(
                weights * slopes, axis=0, keepdims=True
            )
            inverse = 1.0 / total
            delta = weighted * inverse
            prob = weights * inverse
            prob_b = prob.astype(jnp.bfloat16)
            slope_b = (prob * (slopes - delta)).astype(jnp.bfloat16)
            if keep:
                norms[block, 0:1] = factor * inverse
                norms[block, 1:2] = delta
                p_low[block, :span] = prob_b
                s_low[block, :span] = slope_b
            if send:
                if block == 0:
                    far_v, far_k = prob_b[tok:], slope_b[tok:]
                    g_back[pack, 0, 0] = nn(slope_b[:tok], stacked(q_all, pack, 0)).astype(jnp.bfloat16)
                    g_back[pack, 0, 1] = nn(prob_b[:tok], stacked(u_all, pack, 0)).astype(jnp.bfloat16)
                    pl.when(chip != 1)(back_copy(pack, 0).start)
                else:
                    for n, (rows, far, near) in enumerate(((q_all, far_k, slope_b), (u_all, far_v, prob_b))):
                        g_back[pack, 1, n] = nn(
                            jnp.concatenate([far, near], axis=1),
                            jnp.concatenate([stacked(rows, pack, 0), stacked(rows, pack, 1)], axis=0),
                        ).astype(jnp.bfloat16)
                    back_copy(pack, 1).start()
                    pl.when(chip == 1)(back_copy(pack, 0).start)

    def no_boundary(pack):
        for block in range(2):
            inverse = 1.0 / stats[pack, block, 1:2]
            norms[block, 0:1] = inverse
            norms[block, 1:2] = stats[pack, block, 2:3] * inverse
            span = (2 - block) * tok
            p_low[block, :span] = jnp.zeros((span, heads * tok), jnp.bfloat16)
            s_low[block, :span] = jnp.zeros((span, heads * tok), jnp.bfloat16)

    def kv_in(pack):
        for block in range(2):
            remote(
                kv_own.at[0], kv_all.at[pack, block], kv_send.at[0], kv_recv.at[pack, block], mate
            ).wait_recv()

    passed = remote(kv_all.at[0, pl.ds(0, 2)], kv_all.at[0, pl.ds(0, 2)], pass_send, pass_recv, mate)

    for copy in loads[6:]:
        copy.wait()
    for copy in mates(0, peer):
        copy.wait_recv()

    @pl.when(has_later & (core == 1))
    def _():
        kv_out[1].start()


    @pl.when(core == 0)
    def _():
        local_part(0, True)

        @pl.when(has_earlier)
        def _():
            passed.wait_recv()
            boundary_part(0, True, False)

    @pl.when(core == 1)
    def _():
        local_part(0, False)
        for copy in mates(1, 0):
            copy.wait_recv()
        local_part(1, True)

        @pl.when(has_earlier)
        def _():
            kv_in(0)
            passed.start()
            boundary_part(0, False, True)
            kv_in(1)
            boundary_part(1, True, True)

    @pl.when(jnp.logical_not(has_earlier))
    def _():
        no_boundary(core)

    for block in range(2):
        span = (block + 1) * tok
        row = (2 - block) * tok
        prob = e_loc[block, :span] * norms[block, 0:1]
        prob_b = prob.astype(jnp.bfloat16)
        slope_b = (prob * (d_loc[block, :span] - norms[block, 1:2])).astype(jnp.bfloat16)
        p_low[block, row:] = prob_b
        s_low[block, row:] = slope_b
        part_v = nn(prob_b, stacked(u_all, core, block))
        part_k = nn(slope_b, stacked(q_all, core, block))
        if block == 0:
            carry_k, carry_v = part_k, part_v
        else:
            g_mine[0, 0] = carry_k + part_k[:tok]
            g_mine[0, 1] = carry_v + part_v[:tok]
            g_mine[1, 0] = part_k[tok:]
            g_mine[1, 1] = part_v[tok:]
    swap = remote(g_mine.at[peer], g_mate, gm_send, gm_recv, mate)
    swap.start()

    for block in range(2):
        keys = kv_all[core, block : block + 3, 0].reshape(3 * tok, HEAD)
        vals = kv_all[core, block : block + 3, 1].reshape(3 * tok, HEAD)
        out_t = nn(jnp.transpose(vals), p_low[block]).astype(jnp.bfloat16)
        gq_t = (nn(jnp.transpose(keys), s_low[block]) * scale).astype(jnp.bfloat16)
        for h in range(heads):
            cols = slice(h * HEAD, (h + 1) * HEAD)
            rows = slice(h * tok, (h + 1) * tok)
            out_buf[block, :, cols] = jnp.transpose(out_t[:, rows])
            gq_buf[block, :, cols] = jnp.transpose(gq_t[:, rows])
    outs = [
        remote(out_buf.at[peer], out_fin.at[core], o_send.at[0], o_recv.at[0], mate),
        remote(gq_buf.at[peer], gq_fin.at[core], o_send.at[1], o_recv.at[1], mate),
    ]
    stores = [
        pltpu.make_async_copy(out_buf.at[core], out_fin.at[core], store_sem.at[0]),
        pltpu.make_async_copy(gq_buf.at[core], gq_fin.at[core], store_sem.at[1]),
    ]
    for copy in outs + stores:
        copy.start()

    swap.wait_recv()
    for copy in (
        remote(out_buf.at[core], out_fin.at[peer], o_send.at[0], o_recv.at[0], mate),
        remote(gq_buf.at[core], gq_fin.at[peer], o_send.at[1], o_recv.at[1], mate),
    ):
        copy.wait_recv()
    for copy in stores:
        copy.wait()
    for copy in mate_out[0] + outs + [swap]:
        copy.wait_send()

    @pl.when(core == 0)
    def _():
        for copy in mate_out[1]:
            copy.wait_send()

    @pl.when(has_later)
    def _():
        for copy in kv_out:
            copy.wait_send()

    @pl.when(has_earlier & (core == 1))
    def _():
        passed.wait_send()
        for pack in range(2):
            for block in range(2):
                back_copy(pack, block).wait_send()

    mine = g_mine[pl.ds(core, 1)][0]
    for pack in range(2):
        own = core == pack
        sum_k = jnp.where(own, mine[0], g_mate[0])
        sum_v = jnp.where(own, mine[1], g_mate[1])
        pl.when(has_later)(
            remote(
                g_back.at[pack, 0], g_in.at[pack], g_send.at[pack, 0], g_recv.at[pack], mate
            ).wait_recv
        )
        gk_fin[pack] = ((sum_k + g_in[pack, 0].astype(jnp.float32)) * scale).astype(jnp.bfloat16)
        gv_fin[pack] = (sum_v + g_in[pack, 1].astype(jnp.float32)).astype(jnp.bfloat16)


def store(*refs):
    count = (len(refs) - 1) // 2
    copies = [
        pltpu.make_async_copy(refs[i], refs[count + i], refs[-1].at[i]) for i in range(count)
    ]
    for copy in copies:
        copy.start()
    for copy in copies:
        copy.wait()


def per_device(queries, keys, values, upstream, doc_ids):
    packs, tok, features = queries.shape
    heads = features // HEAD
    bf16, f32 = jnp.bfloat16, jnp.float32
    wide = heads * tok
    dma = pltpu.SemaphoreType.DMA
    anywhere = pl.BlockSpec(memory_space=pl.ANY)
    shapes = (queries.shape, queries.shape, keys.shape, keys.shape)
    results = pl.pallas_call(
        kernel,
        out_shape=tuple(pltpu.VMEM(shape, bf16) for shape in shapes),
        in_specs=[anywhere] * 5,
        out_specs=(pl.BlockSpec(memory_space=pltpu.VMEM),) * 4,
        scratch_shapes=[
            pltpu.VMEM((2, 2, tok, features), bf16),
            pltpu.VMEM((2, 2, tok, features), bf16),
            pltpu.VMEM((2, 4, 2, tok, HEAD), bf16),
            pltpu.VMEM((2, 2, tok, HEAD), bf16),
            pltpu.VMEM((2, 4 * tok), jnp.int32),
            pltpu.VMEM((2, 2, 3 * tok, tok), f32),
            pltpu.VMEM((2, 2, 8, wide), f32),
            pltpu.VMEM((2, 8, wide), f32),
            pltpu.VMEM((2, 2 * tok, wide), f32),
            pltpu.VMEM((2, 2 * tok, wide), f32),
            pltpu.VMEM((2, 3 * tok, wide), bf16),
            pltpu.VMEM((2, 3 * tok, wide), bf16),
            pltpu.VMEM((2, 2, 2, tok, HEAD), bf16),
            pltpu.VMEM((2, 2, tok, HEAD), bf16),
            pltpu.VMEM((2, 2, tok, HEAD), f32),
            pltpu.VMEM((2, tok, HEAD), f32),
            pltpu.VMEM((2, tok, features), bf16),
            pltpu.VMEM((2, tok, features), bf16),
            dma((10,)),
            dma((2,)),
            dma((2, 2)),
            dma((2, 3)),
            dma((2, 3)),
            dma(()),
            dma(()),
            dma((2, 2)),
            dma((2,)),
            dma(()),
            dma(()),
            dma((2,)),
            dma((2,)),
            dma((2,)),
        ],
        compiler_params=pltpu.CompilerParams(
            collective_id=0, has_side_effects=True, vmem_limit_bytes=60 * 1024 * 1024
        ),
        name="attention_both_ways",
    )(queries, keys, values, upstream, doc_ids)
    return pl.pallas_call(
        store,
        out_shape=tuple(jax.ShapeDtypeStruct(shape, bf16) for shape in shapes),
        in_specs=[anywhere] * 4,
        out_specs=(anywhere,) * 4,
        scratch_shapes=[dma((4,))],
        compiler_params=pltpu.CompilerParams(vmem_limit_bytes=4 * 1024 * 1024),
        name="store_results",
    )(*results)


def solution(mesh):
    return jax.shard_map(
        per_device,
        mesh=mesh,
        in_specs=(P("dp", "ctx", None),) * 4 + (P("dp", None),),
        out_specs=(P("dp", "ctx", None),) * 4,
        check_vma=False,
    )
```
